128 devices in a mesh: dp: 16 (over z_hi, y, core), seq: 8 (over z_lo, x).
Axes of the slice: x: 4, y: 4, z: 4 (z_hi: 2, z_lo: 2; z = z_hi * 2 + z_lo), core: 2. Of those that a mesh axis runs over, the one named last changes fastest.
Arguments:
- sequence: bfloat16 [16, 2048, 1408], P('dp', 'seq'), may hold values from -6 to 6
- conv_weight: bfloat16 [1408, 5, 1536], P(('dp', 'seq')), may hold values from -0.0625 to 0.0625
- conv_bias: float32 [1536], replicated, may hold values from -3 to 3
- norm_gain: float32 [1536], replicated, may hold values from 0.25 to 1.75
- proj_weight: bfloat16 [1536, 3, 1536], P('dp', None, 'seq'), may hold values from -0.66340347 to 0.66340347
- out_weight: bfloat16 [1536, 1536], P('seq', 'dp'), may hold values from -0.15625 to 0.15625
- cotangent: bfloat16 [16, 1024, 1536], P('dp', 'seq'), may hold values from -6 to 6
Outputs:
- block_out: bfloat16 [16, 1024, 1536], P('dp', 'seq')
- proj_grad: float32 [1536, 3, 1536], P('dp')
- out_grad: float32 [1536, 1536], P('seq')
The draws below stay inside these ranges and needn't reach their ends.
All inputs are finite; a program needn't handle non-finite values.
Results may differ from the reference program's by a relative error of at most 0.0065.
Values may be sent and summed in bfloat16 or wider, within the bound.
No kernel may reach another device: no remote copies, remote signals or barrier semaphores. Data moves between devices by JAX's collectives and lax.ppermute only.
A program may use at most 192 MiB of HBM per device.

```python
import jax
import jax.numpy as jnp
from jax import lax

D = 1536
CIN = 1408
HEADS = 8
HD = 192
KW = 5
LENGTH = 1024
POSITIONS = 2048
SEQS = 16


def draw_proj_weight(key, part):
    key = jax.random.fold_in(key, 11)
    array_shape = (D, 3, D)
    drawn = jnp.clip(jax.random.normal(key, array_shape, jnp.float32), -6.0, 6.0) * D ** (-0.5)
    drawn = jnp.stack([drawn[:, 0, :] * 2.0, drawn[:, 1, :], drawn[:, 2, :]], axis=1)
    return drawn.astype(jnp.bfloat16)


def block_levels(rng, shape, cuts, smallest, top_value):
    def one(dim, blocks):
        draws = jax.random.uniform(jax.random.fold_in(jax.random.fold_in(rng, 6), dim), (blocks,), jnp.float32, smallest / len(cuts), top_value / len(cuts))
        return jnp.repeat(jnp.exp(draws), shape[dim] // blocks).reshape((-1,) + (1,) * (len(shape) - dim - 1))

    loudness = one(*cuts[0])
    for cut in cuts[1:]:
        loudness = loudness * one(*cut)
    return loudness


def scatter_about(key, shape, spread, limit, shards=(), dtype=jnp.bfloat16):
    entries = jax.random.normal(key, shape, jnp.float32) * spread
    if len(shards) > 0:
        entries = block_levels(key, shape, shards, -0.22, 0.18) * entries
    return jnp.clip(entries, min=-limit, max=limit).astype(dtype)


def setup_inputs(seed: int = 0) -> dict:
    seeds = jax.random.split(jax.random.key(seed), 8)
    sequence = scatter_about(seeds[0], (SEQS, POSITIONS, CIN), 1.0, 6.0, ((0, 16), (1, 8)))
    conv_weight = scatter_about(seeds[1], (CIN, KW, D), (CIN * KW) ** -0.5, 0.0625, ((0, 128),))
    conv_bias = scatter_about(seeds[2], (D,), 0.5, 3.0, (), jnp.float32)
    norm_gain = jnp.clip(1.0 + 0.15 * jax.random.normal(seeds[3], (D,), jnp.float32), 0.25, 1.75)
    proj_weight = draw_proj_weight(jax.random.fold_in(seeds[7], 71), 0)
    out_weight = scatter_about(seeds[5], (D, D), D ** -0.5, 0.15625, ((0, 8), (1, 16)))
    cotangent = scatter_about(seeds[6], (SEQS, LENGTH, D), 1.0, 6.0, ((0, 16), (1, 8)))
    return {"sequence": sequence, "conv_weight": conv_weight, "conv_bias": conv_bias, "norm_gain": norm_gain, "proj_weight": proj_weight, "out_weight": out_weight, "cotangent": cotangent}


epsilon = 1e-06

def rounded(values):
    return lax.optimization_barrier(values.astype(jnp.bfloat16))

def widen(values):
    return rounded(values).astype(jnp.float32)

def one_sequence(sequence, cotangent, conv_weight, conv_bias, norm_gain, proj_weight, out_weight):
    conv_reach = KW // 2
    padded = jnp.pad(sequence, ((conv_reach, conv_reach), (0, 0)))
    conv_sum = jnp.zeros((POSITIONS, D), jnp.float32) + conv_bias
    for offset in range(KW):
        conv_sum = conv_sum + jnp.dot(padded[offset:offset + POSITIONS], conv_weight[:, offset, :], preferred_element_type=jnp.float32)
    activated = jax.nn.gelu(conv_sum)
    features = rounded(lax.optimization_barrier(jnp.max(activated.reshape(LENGTH, 2, D), axis=1)))
    widened = features.astype(jnp.float32)
    square_mean = lax.optimization_barrier(jnp.mean(widened * widened, axis=-1, keepdims=True))
    normed = rounded(widened * lax.rsqrt(square_mean + epsilon) * norm_gain)
    query = rounded(jnp.dot(normed, proj_weight[:, 0, :], preferred_element_type=jnp.float32))
    key_rows = rounded(jnp.dot(normed, proj_weight[:, 1, :], preferred_element_type=jnp.float32))
    values = rounded(jnp.dot(normed, proj_weight[:, 2, :], preferred_element_type=jnp.float32))
    q_heads = query.astype(jnp.float32).reshape(LENGTH, HEADS, HD)
    k_heads = key_rows.astype(jnp.float32).reshape(LENGTH, HEADS, HD)
    v_heads = values.astype(jnp.float32).reshape(LENGTH, HEADS, HD)
    inv_scale = HD ** (-0.5)
    scores = jnp.einsum('qhd,khd->hqk', q_heads, k_heads) * inv_scale
    row_top = lax.optimization_barrier(jnp.max(scores, axis=-1, keepdims=True))
    exponent = jnp.exp(scores - row_top)
    weights = exponent / lax.optimization_barrier(jnp.sum(exponent, axis=-1, keepdims=True))
    weights_low = widen(weights)
    mixed = rounded(jnp.einsum('hqk,khd->qhd', weights_low, v_heads)).reshape(LENGTH, D)
    attended = jnp.dot(mixed, out_weight, preferred_element_type=jnp.float32)
    block_out = (widened + attended).astype(jnp.bfloat16)
    out_grad = jnp.dot(mixed.T, cotangent, preferred_element_type=jnp.float32)
    d_mixed = widen(jnp.dot(cotangent, out_weight.T, preferred_element_type=jnp.float32)).reshape(LENGTH, HEADS, HD)
    d_value = rounded(jnp.einsum('hqk,qhd->khd', weights_low, d_mixed))
    d_weights = jnp.einsum('qhd,khd->hqk', d_mixed, v_heads)
    centre = lax.optimization_barrier(jnp.sum(weights * d_weights, axis=-1, keepdims=True))
    d_scores = widen(weights * (d_weights - centre) * inv_scale)
    d_query = rounded(jnp.einsum('hqk,khd->qhd', d_scores, k_heads))
    d_key = rounded(jnp.einsum('hqk,qhd->khd', d_scores, q_heads))
    d_proj = jnp.stack([d_query.reshape(LENGTH, D), d_key.reshape(LENGTH, D), d_value.reshape(LENGTH, D)], axis=1).astype(jnp.float32)
    proj_grad = jnp.einsum('sr,stc->rtc', normed.astype(jnp.float32), d_proj)
    return (block_out, proj_grad, out_grad)

def reference(sequence, conv_weight, conv_bias, norm_gain, proj_weight, out_weight, cotangent):

    def scan_step(totals, inputs_pair):
        block_out, proj_grad, out_grad = one_sequence(inputs_pair[0], inputs_pair[1], conv_weight, conv_bias, norm_gain, proj_weight, out_weight)
        return ((totals[0] + proj_grad, totals[1] + out_grad), block_out)
    initial = (jnp.zeros((D, 3, D), jnp.float32), jnp.zeros((D, D), jnp.float32))
    totals, out_blocks = lax.scan(scan_step, initial, (sequence, cotangent))
    return (out_blocks, totals[0], totals[1])
```

```python
import jax
import jax.numpy as jnp
import numpy as np
from jax import lax
from jax.experimental import pallas as pl
from jax.experimental.pallas import tpu as pltpu
from jax.sharding import Mesh, PartitionSpec as P

HD = 192
D = 1536
NX = 4
CIN = 1408
GROUP = 44
SLOT = 48
PLANE = 32
KPAD = PLANE * SLOT
OUTC = D // NX
KW = 5
EPS = 1e-06
HALO = 16

bf16 = jnp.bfloat16
f32 = jnp.float32


def ring(n, k):
    return [(i, (i + k) % n) for i in range(n)]


def staged_ring(block, axis, cut):
    low = lax.ppermute(block, axis, ring(4, 1))
    high = lax.ppermute(block, axis, ring(4, -1))
    far_a = lax.ppermute(lax.slice_in_dim(low, 0, cut), axis, ring(4, 1))
    far_b = lax.ppermute(lax.slice_in_dim(high, cut, None), axis, ring(4, -1))
    return low, high, far_a, far_b


def conv_kernel(zl_ref, x_ref, *refs):
    (w0, w1, w2, w3a, w3b, o0, o1, o2, o3a, o3b, bias_ref, out_ref, wcat, xs, *accs) = refs
    row = 0
    for ref in (w0, w1, w2, w3a, w3b, o0, o1, o2, o3a, o3b):
        for piece in range(ref.shape[0]):
            for off in range(KW):
                wcat[row : row + SLOT, off * OUTC : (off + 1) * OUTC] = ref[piece, off]
            row += SLOT
    lower = zl_ref[0] == 0
    zeros = jnp.zeros((HALO, KPAD), bf16)
    xs[0:HALO, :] = jnp.where(lower, zeros, x_ref[3, 256 : 256 + HALO, :])
    for b in range(4):
        xs[HALO + b * 256 : HALO + (b + 1) * 256, :] = x_ref[b, 0:256, :]
    xs[HALO + 1024 : 2 * HALO + 1024, :] = jnp.where(lower, x_ref[0, 256 : 256 + HALO, :], zeros)

    @pl.loop(0, 8)
    def _(r):
        base = pl.multiple_of(r * 128, 128)
        y = jnp.dot(xs[pl.ds(base, 128 + 2 * HALO), :], wcat[...], preferred_element_type=f32)
        total = bias_ref[...] + jnp.zeros((128, OUTC), f32)
        for off in range(KW):
            first = HALO + off - 2
            total = total + y[first : first + 128, off * OUTC : (off + 1) * OUTC]
        activated = jax.nn.gelu(total)
        for n, acc in enumerate(accs):
            acc[...] = activated[:, n * 128 : (n + 1) * 128]
            top = jnp.maximum(acc[pl.ds(0, 64, 2), :], acc[pl.ds(1, 64, 2), :])
            out_ref[pl.ds(pl.multiple_of(r * 64, 64), 64), n * 128 : (n + 1) * 128] = top.astype(bf16)


def conv_pool(zl, xblocks, pieces, bias):
    vmem = pl.BlockSpec(memory_space=pltpu.VMEM)
    return pl.pallas_call(
        conv_kernel,
        out_shape=jax.ShapeDtypeStruct((512, OUTC), bf16),
        in_specs=[pl.BlockSpec(memory_space=pltpu.SMEM)] + [vmem] * (len(pieces) + 2),
        out_specs=vmem,
        scratch_shapes=[
            pltpu.VMEM((KPAD, KW * OUTC), bf16),
            pltpu.VMEM((1024 + 2 * HALO, KPAD), bf16),
            *[pltpu.VMEM((128, 128), f32)] * 3,
        ],
        compiler_params=pltpu.CompilerParams(vmem_limit_bytes=48 * 1024 * 1024),
        cost_estimate=pl.CostEstimate(flops=6_000_000_000, bytes_accessed=9_000_000, transcendentals=400_000),
    )(zl, xblocks, *pieces, bias)


VMEM = pl.BlockSpec(memory_space=pltpu.VMEM)
SMEM = pl.BlockSpec(memory_space=pltpu.SMEM)
SCALE = HD ** (-0.5)
WIDE = 256
TOKENS = 1024
BLOCK = 256
NT = (((1,), (1,)), ((), ()))
TN = (((0,), (0,)), ((), ()))


def dot(a, b, dims=(((1,), (0,)), ((), ()))):
    return lax.dot_general(a, b, dims, preferred_element_type=f32)


def softmax_rows(q_block, keys):
    scores = dot(q_block, keys, NT) * SCALE
    exponent = jnp.exp(scores - jnp.max(scores, axis=-1, keepdims=True))
    return exponent * (1.0 / jnp.sum(exponent, axis=-1, keepdims=True))


def forward_kernel(feats_ref, gain_ref, w_ref, normed_ref, qkv_ref, mixed_ref, partial_ref, wq, wo):
    for t in range(3):
        wq[:, t * WIDE : t * WIDE + HD] = w_ref[:, t * HD : (t + 1) * HD]
        wq[:, t * WIDE + HD : (t + 1) * WIDE] = jnp.zeros((D, WIDE - HD), bf16)
    wo[:, :HD] = w_ref[:, 3 * HD :]
    wo[:, HD:] = jnp.zeros((D, WIDE - HD), bf16)

    @pl.loop(0, TOKENS // BLOCK)
    def _(r):
        half, inner = r // 2, pl.multiple_of((r % 2) * BLOCK, BLOCK)
        rows = pl.ds(pl.multiple_of(r * BLOCK, BLOCK), BLOCK)
        total = jnp.zeros((BLOCK, 1), f32)
        for g in range(NX):
            part = feats_ref[half * NX + g, pl.ds(inner, BLOCK), :].astype(f32)
            total = total + jnp.sum(part * part, axis=-1, keepdims=True)
        factor = lax.rsqrt(total * (1.0 / D) + EPS)
        for g in range(NX):
            part = feats_ref[half * NX + g, pl.ds(inner, BLOCK), :].astype(f32)
            lanes = slice(g * OUTC, (g + 1) * OUTC)
            normed_ref[rows, lanes] = (part * factor * gain_ref[:, lanes]).astype(bf16)
        qkv = dot(normed_ref[rows, :], wq[...]).astype(bf16)
        for t in range(3):
            qkv_ref[t, rows, :] = qkv[:, t * WIDE : (t + 1) * WIDE]

    @pl.loop(0, TOKENS // BLOCK)
    def _(r):
        rows = pl.ds(pl.multiple_of(r * BLOCK, BLOCK), BLOCK)
        weights = softmax_rows(qkv_ref[0, rows, :], qkv_ref[1]).astype(bf16)
        mixed = dot(weights, qkv_ref[2]).astype(bf16)
        mixed_ref[rows, :] = mixed
        partial_ref[rows, :] = dot(mixed, wo[...], NT).astype(bf16)


def forward(feats, gain, wfull):
    return pl.pallas_call(
        forward_kernel,
        out_shape=(
            jax.ShapeDtypeStruct((TOKENS, D), bf16),
            jax.ShapeDtypeStruct((3, TOKENS, WIDE), bf16),
            jax.ShapeDtypeStruct((TOKENS, WIDE), bf16),
            jax.ShapeDtypeStruct((TOKENS, D), bf16),
        ),
        in_specs=[VMEM] * 3,
        out_specs=[VMEM] * 4,
        scratch_shapes=[pltpu.VMEM((D, 3 * WIDE), bf16), pltpu.VMEM((D, WIDE), bf16)],
        compiler_params=pltpu.CompilerParams(vmem_limit_bytes=48 * 1024 * 1024),
        cost_estimate=pl.CostEstimate(flops=4_000_000_000, bytes_accessed=16_000_000, transcendentals=1_100_000),
    )(feats, gain, wfull)


def backward_kernel(
    c_ref, qkv_ref, cot_ref, w_ref, normed_ref, mixed_ref, kept_ref, sent_ref, wo, dm, dcat, dk, dv, grads, outs
):
    wo[:, :HD] = w_ref[:, 3 * HD :]
    wo[:, HD:] = jnp.zeros((D, WIDE - HD), bf16)

    @pl.loop(0, TOKENS // BLOCK)
    def _(r):
        rows = pl.ds(pl.multiple_of(r * BLOCK, BLOCK), BLOCK)
        d_mixed = dot(cot_ref[rows, :], wo[...]).astype(bf16)
        q_block = qkv_ref[0, rows, :]
        weights = softmax_rows(q_block, qkv_ref[1])
        d_weights = dot(d_mixed, qkv_ref[2], NT)
        centre = jnp.sum(weights * d_weights, axis=-1, keepdims=True)
        d_scores = (weights * (d_weights - centre) * SCALE).astype(bf16)
        dcat[rows, 0:HD] = dot(d_scores, qkv_ref[1]).astype(bf16)[:, :HD]
        d_value = dot(d_mixed, weights.astype(bf16), TN)
        d_key = dot(q_block, d_scores, TN)

        @pl.when(r == 0)
        def _():
            dv[...] = d_value
            dk[...] = d_key

        @pl.when(r > 0)
        def _():
            dv[...] += d_value
            dk[...] += d_key

    dcat[:, HD : 2 * HD] = dk[...].T.astype(bf16)[:, :HD]
    dcat[:, 2 * HD : 3 * HD] = dv[...].T.astype(bf16)[:, :HD]

    @pl.loop(0, 4)
    def _(n):
        lanes = pl.ds(pl.multiple_of(n * 384, 384), 384)
        grads[lanes, :] = dot(normed_ref[:, lanes], dcat[...], TN)
        outs[:, lanes] = dot(mixed_ref[...], cot_ref[:, lanes], TN)[:HD]

    c = c_ref[0]
    for ref, core in ((kept_ref, c), (sent_ref, 1 - c)):
        for g in range(8):
            rows = pl.ds(pl.multiple_of((2 * g + core) * 96, 96), 96)
            ref[g, :, : 3 * HD] = grads[rows, :].astype(bf16)
            piece = outs[g * 24 : (g + 1) * 24, pl.ds(pl.multiple_of(core * 768, 768), 768)]
            packed = jnp.concatenate([piece[:, j * HD : (j + 1) * HD] for j in range(4)], axis=0)
            ref[g, :, 3 * HD :] = packed.astype(bf16)


def backward(c, qkv, cot, wfull, normed, mixed):
    return pl.pallas_call(
        backward_kernel,
        out_shape=(jax.ShapeDtypeStruct((8, 96, 768), bf16),) * 2,
        in_specs=[SMEM] + [VMEM] * 5,
        out_specs=[VMEM] * 2,
        scratch_shapes=[
            pltpu.VMEM((D, WIDE), bf16),
            pltpu.VMEM((TOKENS, WIDE), bf16),
            pltpu.VMEM((TOKENS, 3 * HD), bf16),
            pltpu.VMEM((WIDE, TOKENS), f32),
            pltpu.VMEM((WIDE, TOKENS), f32),
            pltpu.VMEM((D, 3 * HD), f32),
            pltpu.VMEM((HD, D), f32),
        ],
        compiler_params=pltpu.CompilerParams(vmem_limit_bytes=56 * 1024 * 1024),
        cost_estimate=pl.CostEstimate(flops=6_000_000_000, bytes_accessed=18_000_000, transcendentals=1_100_000),
    )(c, qkv, cot, wfull, normed, mixed)


def total_kernel(parts_ref, proj_ref, out_ref):
    total = parts_ref[0].astype(f32)
    for g in range(1, 8):
        total = total + parts_ref[g].astype(f32)
    proj_ref[...] = total[:, : 3 * HD].astype(bf16)
    packed = total[:, 3 * HD :]
    out_ref[...] = jnp.concatenate([packed[j * 24 : (j + 1) * 24] for j in range(4)], axis=1).astype(bf16)


def total_parts(parts):
    return pl.pallas_call(
        total_kernel,
        out_shape=(jax.ShapeDtypeStruct((96, 3 * HD), bf16), jax.ShapeDtypeStruct((24, 768), bf16)),
        in_specs=[VMEM],
        out_specs=[VMEM] * 2,
    )(parts)


def proj_kernel(heads_ref, out_ref):
    for h in range(8):
        for t in range(3):
            out_ref[t, :, h * HD : (h + 1) * HD] = heads_ref[h, :, t * HD : (t + 1) * HD].astype(f32)


def place_proj(heads):
    return pl.pallas_call(
        proj_kernel,
        out_shape=jax.ShapeDtypeStruct((3, 96, D), f32),
        in_specs=[VMEM],
        out_specs=VMEM,
    )(heads)


def out_kernel(c_ref, own_ref, other_ref, out_ref):
    c = c_ref[0]
    for ref, core in ((own_ref, c), (other_ref, 1 - c)):
        lanes = pl.ds(pl.multiple_of(core * 768, 768), 768)
        for g in range(8):
            out_ref[g * 24 : (g + 1) * 24, lanes] = ref[g].astype(f32)


def place_out(c, own, other):
    return pl.pallas_call(
        out_kernel,
        out_shape=jax.ShapeDtypeStruct((HD, D), f32),
        in_specs=[SMEM, VMEM, VMEM],
        out_specs=VMEM,
    )(c, own, other)


def lane_sources(zh, y, c, zl):
    lane = lax.iota(jnp.int32, KPAD)
    slot, j = lane // SLOT, lane % SLOT
    core = jnp.where(slot < 16, c, 1 - c)
    within = slot % 16
    zstep = within // 4
    ystep = within % 4
    z = zh * 2 + zl
    src_z = (z + jnp.where(zstep == 1, 3, jnp.where(zstep == 2, 1, jnp.where(zstep == 3, 2, 0)))) % 4
    src_y = (y + 4 - ystep) % 4
    plane = (((src_z // 2) * 4 + src_y) * 2 + core) * 2 + src_z % 2
    return jnp.where(j < GROUP, plane * GROUP + j, -1)


def per_device(sequence, conv_weight, conv_bias, norm_gain, proj_weight, out_weight, cotangent):
    zh, y, c, zl, x = (lax.axis_index(a) for a in ("zh", "y", "c", "zl", "x"))
    zring = ("zh", "zl")

    split = conv_weight.reshape(11, KW, NX, OUTC).transpose(2, 1, 0, 3)
    mine = jnp.zeros((NX, KW, 11, OUTC), bf16)
    for k in range(NX):
        piece = lax.dynamic_index_in_dim(split, (x + k) % NX, 0, keepdims=False)
        if k:
            piece = lax.ppermute(piece, "x", ring(NX, k))
        mine = lax.dynamic_update_index_in_dim(mine, piece, (x + NX - k) % NX, 0)
    mine = mine.transpose(1, 0, 2, 3).reshape(KW, GROUP, OUTC)
    mine = jnp.pad(mine, ((0, 0), (0, SLOT - GROUP), (0, 0)))

    sources = lane_sources(zh, y, c, zl)
    select = (lax.broadcasted_iota(jnp.int32, (CIN, KPAD), 0) == sources[None, :]).astype(bf16)
    edge = jnp.where(zl == 0, sequence[0, -HALO:], sequence[0, :HALO])
    edge = lax.ppermute(edge, "zl", ring(2, 1))
    block = jnp.concatenate([sequence[0], edge], axis=0)
    block = jnp.dot(block, select, preferred_element_type=f32).astype(bf16)
    low, high, far_a, far_b = staged_ring(block, "x", 128)
    far = jnp.concatenate([far_a, far_b], axis=0)
    xblocks = jnp.zeros((NX,) + block.shape, bf16)
    for step, part in ((0, block), (3, low), (1, high), (2, far)):
        xblocks = lax.dynamic_update_index_in_dim(xblocks, part, (x + step) % NX, 0)

    ypieces = jnp.stack([mine] + [lax.ppermute(mine, "y", ring(4, k)) for k in (1, 2, 3)])
    zpieces = staged_ring(ypieces, zring, 2)
    pieces = [ypieces, *zpieces]
    pieces = pieces + [lax.ppermute(p, "c", ring(2, 1)) for p in pieces]
    bias = lax.dynamic_slice_in_dim(conv_bias, x * OUTC, OUTC)[None]
    feat = conv_pool(zl.reshape(1), xblocks, pieces, bias)

    wcat = jnp.concatenate([proj_weight.reshape(96, 576), out_weight.T], axis=1)
    wfull = lax.all_gather(wcat, ("zh", "y", "c"), axis=0, tiled=True)
    cot = lax.all_gather(cotangent[0], ("zl", "x"), axis=0, tiled=True)

    feat, cot = lax.optimization_barrier((feat, cot))
    feats = lax.all_to_all(jnp.broadcast_to(feat[None], (8, 512, OUTC)), ("zl", "x"), 0, 0)
    own = feats.reshape(2, NX, 4, 128, OUTC)
    own = lax.dynamic_index_in_dim(own, zl, 0, keepdims=False)
    own = lax.dynamic_index_in_dim(own, x, 1, keepdims=False)
    own = own.transpose(1, 0, 2).reshape(128, D)

    normed, qkv, mixed, partial = forward(feats, norm_gain[None], wfull)
    attended = lax.psum_scatter(partial, ("zl", "x"), scatter_dimension=0, tiled=True)
    block_out = (own.astype(f32) + attended.astype(f32)).astype(bf16)[None]

    core = c.reshape(1)
    kept, sent = backward(core, qkv, cot, wfull, normed, mixed)
    both = (kept.astype(f32) + lax.ppermute(sent, "c", ring(2, 1)).astype(f32)).astype(bf16)
    proj, outs = total_parts(lax.all_to_all(both, ("zh", "y"), 0, 0))

    heads = lax.all_to_all(jnp.broadcast_to(proj[None], (8, 96, 576)), ("zl", "x"), 0, 0)
    rows = lax.all_to_all(jnp.broadcast_to(outs[None], (8, 24, 768)), ("zh", "y"), 0, 0)
    proj_grad = place_proj(heads).transpose(1, 0, 2)
    out_grad = place_out(core, rows, lax.ppermute(rows, "c", ring(2, 1)))
    return (block_out, proj_grad, out_grad)


def solution(mesh):
    fine = Mesh(mesh.devices.reshape(2, 4, 2, 2, 4), ("zh", "y", "c", "zl", "x"))
    dp, seq = ("zh", "y", "c"), ("zl", "x")
    in_specs = (
        P(dp, seq, None),
        P(dp + seq, None, None),
        P(),
        P(),
        P(dp, None, seq),
        P(seq, dp),
        P(dp, seq, None),
    )
    out_specs = (P(dp, seq, None), P(dp, None, None), P(seq, None))
    return jax.shard_map(per_device, mesh=fine, in_specs=in_specs, out_specs=out_specs, check_vma=False)
```

```python
import jax
import jax.numpy as jnp
import numpy as np
from jax import lax
from jax.experimental import pallas as pl
from jax.experimental.pallas import tpu as pltpu
from jax.sharding import Mesh, PartitionSpec as P

HD = 192
D = 1536
NX = 4
CIN = 1408
GROUP = 44
SLOT = 48
PLANE = 32
KPAD = PLANE * SLOT
OUTC = D // NX
KW = 5
EPS = 1e-06
HALO = 16

bf16 = jnp.bfloat16
f32 = jnp.float32


def ring(n, k):
    return [(i, (i + k) % n) for i in range(n)]


def across(low, high, axis, cut):
    far_a = lax.ppermute(lax.slice_in_dim(low, 0, cut), axis, ring(4, 1))
    far_b = lax.ppermute(lax.slice_in_dim(high, cut, None), axis, ring(4, -1))
    return far_a, far_b


def staged_ring(block, axis, cut):
    low = lax.ppermute(block, axis, ring(4, 1))
    high = lax.ppermute(block, axis, ring(4, -1))
    return low, high, *across(low, high, axis, cut)


def conv_kernel(pos_ref, *refs):
    (x0, x1, x2, x3a, x3b, w0, w1, w2, w3a, w3b, o0, o1, o2, o3a, o3b, bias_ref, out_ref, wcat, xs, *accs) = refs
    row = 0
    for ref in (w0, w1, w2, w3a, w3b, o0, o1, o2, o3a, o3b):
        for piece in range(ref.shape[0]):
            for off in range(KW):
                wcat[row : row + SLOT, off * OUTC : (off + 1) * OUTC] = ref[piece, off]
            row += SLOT
    x, half = pos_ref[1], pos_ref[3] % 2
    zeros = jnp.zeros((HALO, KPAD), bf16)
    xs[0:HALO, :] = zeros
    xs[HALO + 1024 : 2 * HALO + 1024, :] = zeros

    def place_halo(b, edge):
        @pl.when(jnp.logical_and(half == 0, b == 0))
        def _():
            xs[HALO + 1024 : 2 * HALO + 1024, :] = edge()

        @pl.when(jnp.logical_and(half == 1, b == 3))
        def _():
            xs[0:HALO, :] = edge()

    for ref, step in ((x0, 0), (x1, 3), (x2, 1)):
        b = (x + step) % NX
        xs[pl.ds(pl.multiple_of(HALO + b * 256, HALO), 256), :] = ref[0:256, :]
        place_halo(b, lambda ref=ref: ref[256 : 256 + HALO, :])
    b = (x + 2) % NX
    xs[pl.ds(pl.multiple_of(HALO + b * 256, HALO), 128), :] = x3a[...]
    xs[pl.ds(pl.multiple_of(HALO + b * 256 + 128, HALO), 128), :] = x3b[0:128, :]
    place_halo(b, lambda: x3b[128 : 128 + HALO, :])

    @pl.loop(0, 4)
    def _(r):
        base = pl.multiple_of(r * 256, 256)
        y = jnp.dot(xs[pl.ds(base, 256 + 2 * HALO), :], wcat[...], preferred_element_type=f32)
        total = bias_ref[...] + jnp.zeros((256, OUTC), f32)
        for off in range(KW):
            first = HALO + off - 2
            total = total + y[first : first + 256, off * OUTC : (off + 1) * OUTC]
        activated = jax.nn.gelu(total)
        for n, acc in enumerate(accs):
            acc[...] = activated[:, n * 128 : (n + 1) * 128]
            top = jnp.maximum(acc[pl.ds(0, 128, 2), :], acc[pl.ds(1, 128, 2), :])
            out_ref[pl.ds(pl.multiple_of(r * 128, 128), 128), n * 128 : (n + 1) * 128] = top.astype(bf16)


VMEM = pl.BlockSpec(memory_space=pltpu.VMEM)
SMEM = pl.BlockSpec(memory_space=pltpu.SMEM)


def conv_pool(pos, xpieces, wpieces, bias):
    return pl.pallas_call(
        conv_kernel,
        out_shape=jax.ShapeDtypeStruct((512, OUTC), bf16),
        in_specs=[SMEM] + [VMEM] * (len(xpieces) + len(wpieces) + 1),
        out_specs=VMEM,
        scratch_shapes=[
            pltpu.VMEM((KPAD, KW * OUTC), bf16),
            pltpu.VMEM((1024 + 2 * HALO, KPAD), bf16),
            *[pltpu.VMEM((256, 128), f32)] * 3,
        ],
        compiler_params=pltpu.CompilerParams(vmem_limit_bytes=48 * 1024 * 1024),
        cost_estimate=pl.CostEstimate(flops=6_000_000_000, bytes_accessed=9_000_000, transcendentals=400_000),
    )(pos, *xpieces, *wpieces, bias)


SCALE = HD ** (-0.5)
WIDE = 256
TOKENS = 1024
BLOCK = 256
NT = (((1,), (1,)), ((), ()))
TN = (((0,), (0,)), ((), ()))


def dot(a, b, dims=(((1,), (0,)), ((), ()))):
    return lax.dot_general(a, b, dims, preferred_element_type=f32)


def softmax_rows(q_block, keys):
    scores = dot(q_block, keys, NT) * SCALE
    exponent = jnp.exp(scores - jnp.max(scores, axis=-1, keepdims=True))
    return exponent * (1.0 / jnp.sum(exponent, axis=-1, keepdims=True))


def forward_kernel(pos_ref, *refs):
    feat_refs, refs = refs[:10], refs[10:]
    (gain_ref, z0, z1, z2, z3a, z3b, cot_ref) = refs[:7]
    (normed_ref, qkv_ref, dm_ref, partial_ref, own_ref, sent_ref, wo, feats, wq, mixed_ref, dv, dval, grads, outs) = refs[7:]
    c, x, y, z = (pos_ref[i] for i in range(4))
    for t in range(3):
        wq[:, t * WIDE + HD : (t + 1) * WIDE] = jnp.zeros((D, WIDE - HD), bf16)
    wo[:, HD:] = jnp.zeros((D, WIDE - HD), bf16)
    for ref, zstep, first in ((z0, 0, 0), (z1, 3, 0), (z2, 1, 0), (z3a, 2, 0), (z3b, 2, 2)):
        for k in range(ref.shape[0]):
            src_z, src_y = (z + zstep) % 4, (y + 4 - (first + k)) % 4
            rows = pl.ds(pl.multiple_of((((src_z // 2) * 4 + src_y) * 2 + src_z % 2) * 96, 96), 96)
            piece = ref[k]
            for t in range(3):
                wq[rows, t * WIDE : t * WIDE + HD] = piece[:, t * HD : (t + 1) * HD]
            wo[rows, :HD] = piece[:, 3 * HD :]

    for side in range(2):
        half = c if side == 0 else 1 - c
        for ref, step, first in zip(feat_refs[side * 5 : side * 5 + 5], (0, 3, 1, 2, 2), (0, 0, 0, 0, 256)):
            size = ref.shape[0]
            rows = pl.ds(pl.multiple_of(half * 512 + first, 256), size)
            lanes = pl.ds(pl.multiple_of(((x + step) % NX) * OUTC, 128), OUTC)
            feats[rows, lanes] = ref[...]
    own_ref[...] = feats[pl.ds(pl.multiple_of((c * NX + x) * 128, 128), 128), :]

    @pl.loop(0, TOKENS // BLOCK)
    def _(r):
        rows = pl.ds(pl.multiple_of(r * BLOCK, BLOCK), BLOCK)
        part = feats[rows, :].astype(f32)
        factor = lax.rsqrt(jnp.sum(part * part, axis=-1, keepdims=True) * (1.0 / D) + EPS)
        normed = (part * factor * gain_ref[...]).astype(bf16)
        normed_ref[rows, :] = normed
        qkv = dot(normed, wq[...]).astype(bf16)
        for t in range(3):
            qkv_ref[t, rows, :] = qkv[:, t * WIDE : (t + 1) * WIDE]

    @pl.loop(0, TOKENS // BLOCK)
    def _(r):
        rows = pl.ds(pl.multiple_of(r * BLOCK, BLOCK), BLOCK)
        weights = softmax_rows(qkv_ref[0, rows, :], qkv_ref[1]).astype(bf16)
        mixed = dot(weights, qkv_ref[2]).astype(bf16)
        mixed_ref[rows, :] = mixed
        partial_ref[rows, :] = dot(mixed, wo[...], NT).astype(bf16)
        d_mixed = dot(cot_ref[rows, :], wo[...]).astype(bf16)
        dm_ref[rows, :] = d_mixed
        d_value = dot(d_mixed, weights, TN)

        @pl.when(r == 0)
        def _():
            dv[...] = d_value

        @pl.when(r > 0)
        def _():
            dv[...] += d_value

    dval[...] = dv[...].T.astype(bf16)

    @pl.loop(0, 4)
    def _(n):
        lanes = pl.ds(pl.multiple_of(n * 384, 384), 384)
        grads[lanes, :] = dot(normed_ref[:, lanes], dval[...], TN)
        outs[:, lanes] = dot(mixed_ref[...], cot_ref[:, lanes], TN)[:HD]

    for d in range(16):
        sent_ref[d, :, :HD] = grads[d * 96 : (d + 1) * 96, :HD].astype(bf16)
        g, lane = d // 2, (d % 2) * 768
        packed = [outs[g * 24 : (g + 1) * 24, lane + j * HD : lane + (j + 1) * HD] for j in range(4)]
        sent_ref[d, :, HD:] = jnp.concatenate(packed, axis=0).astype(bf16)


def forward(pos, feats, gain, wpieces, cot):
    return pl.pallas_call(
        forward_kernel,
        out_shape=(
            jax.ShapeDtypeStruct((TOKENS, D), bf16),
            jax.ShapeDtypeStruct((3, TOKENS, WIDE), bf16),
            jax.ShapeDtypeStruct((TOKENS, WIDE), bf16),
            jax.ShapeDtypeStruct((TOKENS, D), bf16),
            jax.ShapeDtypeStruct((128, D), bf16),
            jax.ShapeDtypeStruct((16, 96, 2 * HD), bf16),
        ),
        in_specs=[SMEM] + [VMEM] * 17,
        out_specs=[VMEM] * 6,
        scratch_shapes=[
            pltpu.VMEM((D, WIDE), bf16),
            pltpu.VMEM((TOKENS, D), bf16),
            pltpu.VMEM((D, 3 * WIDE), bf16),
            pltpu.VMEM((TOKENS, WIDE), bf16),
            pltpu.VMEM((WIDE, TOKENS), f32),
            pltpu.VMEM((TOKENS, WIDE), bf16),
            pltpu.VMEM((D, WIDE), f32),
            pltpu.VMEM((HD, D), f32),
        ],
        compiler_params=pltpu.CompilerParams(vmem_limit_bytes=56 * 1024 * 1024),
        cost_estimate=pl.CostEstimate(flops=8_000_000_000, bytes_accessed=20_000_000, transcendentals=1_100_000),
    )(pos, *feats, gain, *wpieces, cot)


def backward_kernel(qkv_ref, dm_ref, normed_ref, sent_ref, dcat, dk, grads):
    @pl.loop(0, TOKENS // BLOCK)
    def _(r):
        rows = pl.ds(pl.multiple_of(r * BLOCK, BLOCK), BLOCK)
        q_block = qkv_ref[0, rows, :]
        weights = softmax_rows(q_block, qkv_ref[1])
        d_weights = dot(dm_ref[rows, :], qkv_ref[2], NT)
        centre = jnp.sum(weights * d_weights, axis=-1, keepdims=True)
        d_scores = (weights * (d_weights - centre) * SCALE).astype(bf16)
        dcat[rows, 0:HD] = dot(d_scores, qkv_ref[1]).astype(bf16)[:, :HD]
        d_key = dot(q_block, d_scores, TN)

        @pl.when(r == 0)
        def _():
            dk[...] = d_key

        @pl.when(r > 0)
        def _():
            dk[...] += d_key

    dcat[:, HD:] = dk[...].T.astype(bf16)[:, :HD]

    @pl.loop(0, 4)
    def _(n):
        lanes = pl.ds(pl.multiple_of(n * 384, 384), 384)
        grads[lanes, :] = dot(normed_ref[:, lanes], dcat[...], TN)

    for d in range(16):
        sent_ref[d] = grads[d * 96 : (d + 1) * 96, :].astype(bf16)


def backward(qkv, d_mixed, normed):
    return pl.pallas_call(
        backward_kernel,
        out_shape=jax.ShapeDtypeStruct((16, 96, 2 * HD), bf16),
        in_specs=[VMEM] * 3,
        out_specs=VMEM,
        scratch_shapes=[
            pltpu.VMEM((TOKENS, 2 * HD), bf16),
            pltpu.VMEM((WIDE, TOKENS), f32),
            pltpu.VMEM((D, 2 * HD), f32),
        ],
        compiler_params=pltpu.CompilerParams(vmem_limit_bytes=56 * 1024 * 1024),
        cost_estimate=pl.CostEstimate(flops=6_000_000_000, bytes_accessed=8_000_000, transcendentals=1_100_000),
    )(qkv, d_mixed, normed)


def total_kernel(parts_ref, out_ref):
    total = parts_ref[0].astype(f32)
    for g in range(1, 16):
        total = total + parts_ref[g].astype(f32)
    out_ref[...] = total.astype(bf16)


def total_parts(parts):
    return pl.pallas_call(
        total_kernel,
        out_shape=jax.ShapeDtypeStruct((96, 2 * HD), bf16),
        in_specs=[VMEM],
        out_specs=VMEM,
    )(parts)


def proj_kernel(heads_ref, out_ref):
    for h in range(8):
        for t in range(3):
            out_ref[t, :, h * HD : (h + 1) * HD] = heads_ref[h, :, t * HD : (t + 1) * HD].astype(f32)


def place_proj(heads):
    return pl.pallas_call(
        proj_kernel,
        out_shape=jax.ShapeDtypeStruct((3, 96, D), f32),
        in_specs=[VMEM],
        out_specs=VMEM,
    )(heads)


def out_kernel(pos_ref, own_ref, other_ref, out_ref):
    c, y, zh = pos_ref[0], pos_ref[2], pos_ref[3] // 2
    for ref, core in ((own_ref, c), (other_ref, 1 - c)):
        lanes = pl.ds(pl.multiple_of(core * 768, 768), 768)
        for step in range(2):
            for k in range(4):
                g = ((zh + step) % 2) * 4 + (y + 4 - k) % 4
                piece = [ref[step, k, j * 24 : (j + 1) * 24, :] for j in range(4)]
                rows = pl.ds(pl.multiple_of(g * 24, 8), 24)
                out_ref[rows, lanes] = jnp.concatenate(piece, axis=1).astype(f32)


def place_out(c, own, other):
    return pl.pallas_call(
        out_kernel,
        out_shape=jax.ShapeDtypeStruct((HD, D), f32),
        in_specs=[SMEM, VMEM, VMEM],
        out_specs=VMEM,
    )(c, own, other)


def lane_sources(zh, y, c, zl):
    lane = lax.iota(jnp.int32, KPAD)
    slot, j = lane // SLOT, lane % SLOT
    core = jnp.where(slot < 16, c, 1 - c)
    within = slot % 16
    zstep = within // 4
    ystep = within % 4
    z = zh * 2 + zl
    src_z = (z + jnp.where(zstep == 1, 3, jnp.where(zstep == 2, 1, jnp.where(zstep == 3, 2, 0)))) % 4
    src_y = (y + 4 - ystep) % 4
    plane = (((src_z // 2) * 4 + src_y) * 2 + core) * 2 + src_z % 2
    return jnp.where(j < GROUP, plane * GROUP + j, -1)


def lanes_kernel(block_ref, edge_ref, sources_ref, out_ref):
    for n in range(4):
        lanes = slice(n * 384, (n + 1) * 384)
        select = lax.broadcasted_iota(jnp.int32, (CIN, 384), 0) == sources_ref[:, lanes]
        select = jnp.where(select, 1.0, 0.0).astype(bf16)
        out_ref[0:256, lanes] = dot(block_ref[...], select).astype(bf16)
        out_ref[256:, lanes] = dot(edge_ref[...], select).astype(bf16)


def order_lanes(block, edge, sources):
    return pl.pallas_call(
        lanes_kernel,
        out_shape=jax.ShapeDtypeStruct((256 + HALO, KPAD), bf16),
        in_specs=[VMEM] * 3,
        out_specs=VMEM,
        compiler_params=pltpu.CompilerParams(vmem_limit_bytes=32 * 1024 * 1024),
        cost_estimate=pl.CostEstimate(flops=1_200_000_000, bytes_accessed=1_600_000, transcendentals=0),
    )(block, edge, sources)


def swap_axes(value):
    return lax.ppermute(value, ("c", "zl"), [(0, 0), (1, 2), (2, 1), (3, 3)])


def from_other_core(parts):
    return [lax.ppermute(p, "c", ring(2, 1)) for p in parts]


def per_device(sequence, conv_weight, conv_bias, norm_gain, proj_weight, out_weight, cotangent):
    zh, y, c, zl, x = (lax.axis_index(a) for a in ("zh", "y", "c", "zl", "x"))
    zring = ("zh", "zl")
    pos = jnp.stack([c, x, y, zh * 2 + zl])

    edge = jnp.where(zl == 0, sequence[0, -HALO:], sequence[0, :HALO])
    edge = lax.ppermute(edge, "zl", ring(2, 1))
    block = order_lanes(sequence[0], edge, lane_sources(zh, y, c, zl)[None])

    split = conv_weight.reshape(11, KW, NX, OUTC).transpose(2, 1, 0, 3)
    mine = jnp.zeros((NX, KW, 11, OUTC), bf16)
    for k in range(NX):
        piece = lax.dynamic_index_in_dim(split, (x + k) % NX, 0, keepdims=False)
        if k:
            piece = lax.ppermute(piece, "x", ring(NX, k))
        mine = lax.dynamic_update_index_in_dim(mine, piece, (x + NX - k) % NX, 0)
    mine = mine.transpose(1, 0, 2, 3).reshape(KW, GROUP, OUTC)
    mine = jnp.pad(mine, ((0, 0), (0, SLOT - GROUP), (0, 0)))

    later = jnp.concatenate([proj_weight.reshape(96, 3 * HD), out_weight.T], axis=1).reshape(48, D)
    later = swap_axes(jnp.concatenate([cotangent[0], later], axis=0))

    block, mine = lax.optimization_barrier((block, mine))
    ypieces = [mine] + [lax.ppermute(mine, "y", ring(4, k)) for k in (1, 2, 3)]
    *ypieces, block, later = lax.optimization_barrier((*ypieces, block, later))
    ypieces = jnp.stack(ypieces)
    head_w = later[128:].reshape(96, 768)
    xlow, xhigh = (lax.ppermute(block, "x", ring(4, k)) for k in (1, -1))
    zlow, zhigh = (lax.ppermute(ypieces, zring, ring(4, k)) for k in (1, -1))
    head_w = jnp.stack([head_w] + [lax.ppermute(head_w, "y", ring(4, k)) for k in (1, 2, 3)])
    xlow, xhigh, zlow, zhigh, head_w = lax.optimization_barrier((xlow, xhigh, zlow, zhigh, head_w))
    xfar = across(xlow, xhigh, "x", 128)
    zfar = across(zlow, zhigh, zring, 2)
    *xfar, za, zb, head_w, cot = lax.optimization_barrier((*xfar, *zfar, head_w, later[:128]))
    cot = lax.all_gather(cot, ("c", "x"), axis=0, tiled=True)
    xpieces = [block, xlow, xhigh, *xfar]
    wpieces = [ypieces, zlow, zhigh, za, zb]
    head_w = [head_w, *staged_ring(head_w, zring, 2)]
    bias = lax.dynamic_slice_in_dim(conv_bias, x * OUTC, OUTC)[None]

    feat = swap_axes(conv_pool(pos, xpieces, wpieces + from_other_core(wpieces), bias))
    feats = [feat, *staged_ring(feat, "x", 256)]
    feats = feats + from_other_core(feats)

    plane = ("zh", "y", "zl")
    normed, qkv, d_mixed, partial, own, first = forward(pos, feats, norm_gain[None], head_w, cot)
    attended = lax.psum_scatter(partial, ("c", "x"), scatter_dimension=0, tiled=True)
    first = lax.all_to_all(first, plane, 0, 0)
    second = backward(qkv, d_mixed, normed)
    first, second = lax.optimization_barrier((first, second))
    second = lax.all_to_all(second, plane, 0, 0)
    first = swap_axes(total_parts(first))
    rows = jnp.stack([first[:, HD:]] + [lax.ppermute(first[:, HD:], "y", ring(4, k)) for k in (1, 2, 3)])

    block_out = swap_axes((own.astype(f32) + attended.astype(f32)).astype(bf16))
    second, rows, block_out = lax.optimization_barrier((second, rows, block_out))
    second = swap_axes(total_parts(second))
    rows = jnp.stack([rows, lax.ppermute(rows, "zh", ring(2, 1))])
    proj = jnp.concatenate([second, first[:, :HD]], axis=1)
    heads = lax.all_to_all(jnp.broadcast_to(proj[None], (8, 96, 3 * HD)), ("zl", "x"), 0, 0)
    proj_grad = place_proj(heads).transpose(1, 0, 2)
    out_grad = place_out(pos, rows, lax.ppermute(rows, "c", ring(2, 1)))
    return (block_out[None], proj_grad, out_grad)


def solution(mesh):
    fine = Mesh(mesh.devices.reshape(2, 4, 2, 2, 4), ("zh", "y", "c", "zl", "x"))
    dp, seq = ("zh", "y", "c"), ("zl", "x")
    in_specs = (
        P(dp, seq, None),
        P(dp + seq, None, None),
        P(),
        P(),
        P(dp, None, seq),
        P(seq, dp),
        P(dp, seq, None),
    )
    out_specs = (P(dp, seq, None), P(dp, None, None), P(seq, None))
    return jax.shard_map(per_device, mesh=fine, in_specs=in_specs, out_specs=out_specs, check_vma=False)
```

```python
import jax
import jax.numpy as jnp
import numpy as np
from jax import lax
from jax.experimental import pallas as pl
from jax.experimental.pallas import tpu as pltpu
from jax.sharding import Mesh, PartitionSpec as P

HD = 192
D = 1536
NX = 4
CIN = 1408
GROUP = 44
SLOT = 48
PLANE = 32
KPAD = PLANE * SLOT
OUTC = D // NX
KW = 5
EPS = 1e-06
HALO = 16
ROWS = 512

bf16 = jnp.bfloat16
f32 = jnp.float32


def ring(n, k):
    return [(i, (i + k) % n) for i in range(n)]


def across(low, high, axis, cut):
    far_a = lax.ppermute(lax.slice_in_dim(low, 0, cut), axis, ring(4, 1))
    far_b = lax.ppermute(lax.slice_in_dim(high, cut, None), axis, ring(4, -1))
    return far_a, far_b


def staged_ring(block, axis, cut):
    low = lax.ppermute(block, axis, ring(4, 1))
    high = lax.ppermute(block, axis, ring(4, -1))
    return low, high, *across(low, high, axis, cut)


def conv_kernel(pos_ref, *refs):
    (x0, x1, x2, x3a, x3b, w0, w1, w2, w3, o0, o1, o2, o3, bias_ref, out_ref, wcat, xs, *accs) = refs
    row = 0
    for ref in (w0, w1, w2, w3, o0, o1, o2, o3):
        for piece in range(ref.shape[0]):
            for off in range(KW):
                wcat[row : row + SLOT, off * OUTC : (off + 1) * OUTC] = ref[piece, off]
            row += SLOT
    x, half = pos_ref[1], pos_ref[3] % 2
    zeros = jnp.zeros((HALO, KPAD), bf16)
    xs[0:HALO, :] = zeros
    xs[HALO + 1024 : 2 * HALO + 1024, :] = zeros

    def place_halo(b, edge):
        @pl.when(jnp.logical_and(half == 0, b == 0))
        def _():
            xs[HALO + 1024 : 2 * HALO + 1024, :] = edge()

        @pl.when(jnp.logical_and(half == 1, b == 3))
        def _():
            xs[0:HALO, :] = edge()

    for ref, step in ((x0, 0), (x1, 3), (x2, 1)):
        b = (x + step) % NX
        xs[pl.ds(pl.multiple_of(HALO + b * 256, HALO), 256), :] = ref[0:256, :]
        place_halo(b, lambda ref=ref: ref[256 : 256 + HALO, :])
    b = (x + 2) % NX
    xs[pl.ds(pl.multiple_of(HALO + b * 256, HALO), 128), :] = x3a[...]
    xs[pl.ds(pl.multiple_of(HALO + b * 256 + 128, HALO), 128), :] = x3b[0:128, :]
    place_halo(b, lambda: x3b[128 : 128 + HALO, :])

    @pl.loop(0, 1024 // ROWS)
    def _(r):
        base = pl.multiple_of(r * ROWS, ROWS)
        y = jnp.dot(xs[pl.ds(base, ROWS + 2 * HALO), :], wcat[...], preferred_element_type=f32)
        total = bias_ref[...] + jnp.zeros((ROWS, OUTC), f32)
        for off in range(KW):
            first = HALO + off - 2
            total = total + y[first : first + ROWS, off * OUTC : (off + 1) * OUTC]
        activated = jax.nn.gelu(total)
        for n, acc in enumerate(accs):
            acc[...] = activated[:, n * 128 : (n + 1) * 128]
            top = jnp.maximum(acc[pl.ds(0, ROWS // 2, 2), :], acc[pl.ds(1, ROWS // 2, 2), :])
            out_ref[pl.ds(pl.multiple_of(r * (ROWS // 2), ROWS // 2), ROWS // 2), n * 128 : (n + 1) * 128] = top.astype(bf16)


VMEM = pl.BlockSpec(memory_space=pltpu.VMEM)
SMEM = pl.BlockSpec(memory_space=pltpu.SMEM)


def conv_pool(pos, xpieces, wpieces, bias):
    return pl.pallas_call(
        conv_kernel,
        out_shape=jax.ShapeDtypeStruct((512, OUTC), bf16),
        in_specs=[SMEM] + [VMEM] * (len(xpieces) + len(wpieces) + 1),
        out_specs=VMEM,
        scratch_shapes=[
            pltpu.VMEM((KPAD, KW * OUTC), bf16),
            pltpu.VMEM((1024 + 2 * HALO, KPAD), bf16),
            *[pltpu.VMEM((ROWS, 128), f32)] * 3,
        ],
        compiler_params=pltpu.CompilerParams(vmem_limit_bytes=48 * 1024 * 1024),
        cost_estimate=pl.CostEstimate(flops=6_000_000_000, bytes_accessed=9_000_000, transcendentals=400_000),
    )(pos, *xpieces, *wpieces, bias)


SCALE = HD ** (-0.5)
WIDE = 256
TOKENS = 1024
BLOCK = 512
NT = (((1,), (1,)), ((), ()))
TN = (((0,), (0,)), ((), ()))


def dot(a, b, dims=(((1,), (0,)), ((), ()))):
    return lax.dot_general(a, b, dims, preferred_element_type=f32)


def softmax_rows(q_block, keys):
    scores = dot(q_block, keys, NT) * SCALE
    exponent = jnp.exp(scores - jnp.max(scores, axis=-1, keepdims=True))
    return exponent * (1.0 / jnp.sum(exponent, axis=-1, keepdims=True))


def forward_kernel(pos_ref, *refs):
    feat_refs, refs = refs[:10], refs[10:]
    (gain_ref, z0, z1, z2, z3a, z3b, normed_ref, qkv_ref, mixed_ref, partial_ref, own_ref, wo, feats, wq) = refs
    c, x, z = pos_ref[0], pos_ref[1], pos_ref[3]
    for t in range(3):
        wq[:, t * WIDE + HD : (t + 1) * WIDE] = jnp.zeros((D, WIDE - HD), bf16)
    wo[:, HD:] = jnp.zeros((D, WIDE - HD), bf16)
    for ref, zstep, first in ((z0, 0, 0), (z1, 3, 0), (z2, 1, 0), (z3a, 2, 0), (z3b, 2, 2)):
        for k in range(ref.shape[0]):
            src_z, src_y = (z + zstep) % 4, first + k
            rows = pl.ds(pl.multiple_of((((src_z // 2) * 4 + src_y) * 2 + src_z % 2) * 96, 96), 96)
            piece = ref[k]
            for t in range(3):
                wq[rows, t * WIDE : t * WIDE + HD] = piece[:, t * HD : (t + 1) * HD]
            wo[rows, :HD] = piece[:, 3 * HD :]

    for side in range(2):
        half = c if side == 0 else 1 - c
        for ref, step, first in zip(feat_refs[side * 5 : side * 5 + 5], (0, 3, 1, 2, 2), (0, 0, 0, 0, 256)):
            size = ref.shape[0]
            rows = pl.ds(pl.multiple_of(half * 512 + first, 256), size)
            lanes = pl.ds(pl.multiple_of(((x + step) % NX) * OUTC, 128), OUTC)
            feats[rows, lanes] = ref[...]
    own_ref[...] = feats[pl.ds(pl.multiple_of((c * NX + x) * 128, 128), 128), :]

    @pl.loop(0, TOKENS // BLOCK)
    def _(r):
        rows = pl.ds(pl.multiple_of(r * BLOCK, BLOCK), BLOCK)
        part = feats[rows, :].astype(f32)
        factor = lax.rsqrt(jnp.sum(part * part, axis=-1, keepdims=True) * (1.0 / D) + EPS)
        normed = (part * factor * gain_ref[...]).astype(bf16)
        normed_ref[rows, :] = normed
        qkv = dot(normed, wq[...]).astype(bf16)
        for t in range(3):
            qkv_ref[t, rows, :] = qkv[:, t * WIDE : (t + 1) * WIDE]

    @pl.loop(0, TOKENS // BLOCK)
    def _(r):
        rows = pl.ds(pl.multiple_of(r * BLOCK, BLOCK), BLOCK)
        weights = softmax_rows(qkv_ref[0, rows, :], qkv_ref[1]).astype(bf16)
        mixed = dot(weights, qkv_ref[2]).astype(bf16)
        mixed_ref[rows, :] = mixed
        partial_ref[rows, :] = dot(mixed, wo[...], NT).astype(bf16)


def forward(pos, feats, gain, wpieces):
    return pl.pallas_call(
        forward_kernel,
        out_shape=(
            jax.ShapeDtypeStruct((TOKENS, D), bf16),
            jax.ShapeDtypeStruct((3, TOKENS, WIDE), bf16),
            jax.ShapeDtypeStruct((TOKENS, WIDE), bf16),
            jax.ShapeDtypeStruct((TOKENS, D), bf16),
            jax.ShapeDtypeStruct((128, D), bf16),
            jax.ShapeDtypeStruct((D, WIDE), bf16),
        ),
        in_specs=[SMEM] + [VMEM] * 16,
        out_specs=[VMEM] * 6,
        scratch_shapes=[pltpu.VMEM((TOKENS, D), bf16), pltpu.VMEM((D, 3 * WIDE), bf16)],
        compiler_params=pltpu.CompilerParams(vmem_limit_bytes=48 * 1024 * 1024),
        cost_estimate=pl.CostEstimate(flops=4_000_000_000, bytes_accessed=16_000_000, transcendentals=1_100_000),
    )(pos, *feats, gain, *wpieces)


def backward_kernel(
    qkv_ref, cot_ref, wo, normed_ref, mixed_ref, sent_ref, dcat, dk, dv, grads, outs
):
    @pl.loop(0, TOKENS // BLOCK)
    def _(r):
        rows = pl.ds(pl.multiple_of(r * BLOCK, BLOCK), BLOCK)
        d_mixed = dot(cot_ref[rows, :], wo[...]).astype(bf16)
        q_block = qkv_ref[0, rows, :]
        weights = softmax_rows(q_block, qkv_ref[1])
        d_weights = dot(d_mixed, qkv_ref[2], NT)
        centre = jnp.sum(weights * d_weights, axis=-1, keepdims=True)
        d_scores = (weights * (d_weights - centre) * SCALE).astype(bf16)
        dcat[rows, 0:HD] = dot(d_scores, qkv_ref[1]).astype(bf16)[:, :HD]
        d_value = dot(d_mixed, weights.astype(bf16), TN)
        d_key = dot(q_block, d_scores, TN)

        @pl.when(r == 0)
        def _():
            dv[...] = d_value
            dk[...] = d_key

        @pl.when(r > 0)
        def _():
            dv[...] += d_value
            dk[...] += d_key

    dcat[:, HD : 2 * HD] = dk[...].T.astype(bf16)[:, :HD]
    dcat[:, 2 * HD : 3 * HD] = dv[...].T.astype(bf16)[:, :HD]

    @pl.loop(0, 4)
    def _(n):
        lanes = pl.ds(pl.multiple_of(n * 384, 384), 384)
        grads[lanes, :] = dot(normed_ref[:, lanes], dcat[...], TN)
        outs[:, lanes] = dot(mixed_ref[...], cot_ref[:, lanes], TN)[:HD]

    for d in range(16):
        sent_ref[d, :, : 3 * HD] = grads[d * 96 : (d + 1) * 96, :].astype(bf16)
        g, lane = d // 2, (d % 2) * 768
        packed = [outs[g * 24 : (g + 1) * 24, lane + j * HD : lane + (j + 1) * HD] for j in range(4)]
        sent_ref[d, :, 3 * HD :] = jnp.concatenate(packed, axis=0).astype(bf16)


def backward(qkv, cot, wo, normed, mixed):
    return pl.pallas_call(
        backward_kernel,
        out_shape=jax.ShapeDtypeStruct((16, 96, 768), bf16),
        in_specs=[VMEM] * 5,
        out_specs=VMEM,
        scratch_shapes=[
            pltpu.VMEM((TOKENS, 3 * HD), bf16),
            pltpu.VMEM((WIDE, TOKENS), f32),
            pltpu.VMEM((WIDE, TOKENS), f32),
            pltpu.VMEM((D, 3 * HD), f32),
            pltpu.VMEM((HD, D), f32),
        ],
        compiler_params=pltpu.CompilerParams(vmem_limit_bytes=56 * 1024 * 1024),
        cost_estimate=pl.CostEstimate(flops=6_000_000_000, bytes_accessed=18_000_000, transcendentals=1_100_000),
    )(qkv, cot, wo, normed, mixed)


def total_kernel(parts_ref, out_ref):
    total = parts_ref[0].astype(f32)
    for g in range(1, 16):
        total = total + parts_ref[g].astype(f32)
    out_ref[...] = total.astype(bf16)


def total_parts(parts):
    return pl.pallas_call(
        total_kernel,
        out_shape=jax.ShapeDtypeStruct((96, 768), bf16),
        in_specs=[VMEM],
        out_specs=VMEM,
    )(parts)


def proj_kernel(heads_ref, out_ref):
    for h in range(8):
        for t in range(3):
            out_ref[t, :, h * HD : (h + 1) * HD] = heads_ref[h, :, t * HD : (t + 1) * HD].astype(f32)


def place_proj(heads):
    return pl.pallas_call(
        proj_kernel,
        out_shape=jax.ShapeDtypeStruct((3, 96, D), f32),
        in_specs=[VMEM],
        out_specs=VMEM,
    )(heads)


def out_kernel(pos_ref, own_ref, other_ref, out_ref):
    c, y, zh = pos_ref[0], pos_ref[2], pos_ref[3] // 2
    for ref, core in ((own_ref, c), (other_ref, 1 - c)):
        lanes = pl.ds(pl.multiple_of(core * 768, 768), 768)
        for step in range(2):
            for k in range(4):
                g = ((zh + step) % 2) * 4 + (y + 4 - k) % 4
                piece = [ref[k, step, j * 24 : (j + 1) * 24, :] for j in range(4)]
                rows = pl.ds(pl.multiple_of(g * 24, 8), 24)
                out_ref[rows, lanes] = jnp.concatenate(piece, axis=1).astype(f32)


def place_out(pos, own, other):
    return pl.pallas_call(
        out_kernel,
        out_shape=jax.ShapeDtypeStruct((HD, D), f32),
        in_specs=[SMEM, VMEM, VMEM],
        out_specs=VMEM,
    )(pos, own, other)


def lane_sources(zh, y, c, zl):
    lane = lax.iota(jnp.int32, KPAD)
    slot, j = lane // SLOT, lane % SLOT
    core = jnp.where(slot < 16, c, 1 - c)
    within = slot % 16
    zstep = within // 4
    ystep = within % 4
    z = zh * 2 + zl
    src_z = (z + jnp.where(zstep == 1, 3, jnp.where(zstep == 2, 1, jnp.where(zstep == 3, 2, 0)))) % 4
    src_y = (y + 4 - ystep) % 4
    plane = (((src_z // 2) * 4 + src_y) * 2 + core) * 2 + src_z % 2
    return jnp.where(j < GROUP, plane * GROUP + j, -1)


def lanes_kernel(block_ref, edge_ref, sources_ref, out_ref):
    for n in range(4):
        lanes = slice(n * 384, (n + 1) * 384)
        select = lax.broadcasted_iota(jnp.int32, (CIN, 384), 0) == sources_ref[:, lanes]
        select = jnp.where(select, 1.0, 0.0).astype(bf16)
        out_ref[0:256, lanes] = dot(block_ref[...], select).astype(bf16)
        out_ref[256:, lanes] = dot(edge_ref[...], select).astype(bf16)


def order_lanes(block, edge, sources):
    return pl.pallas_call(
        lanes_kernel,
        out_shape=jax.ShapeDtypeStruct((256 + HALO, KPAD), bf16),
        in_specs=[VMEM] * 3,
        out_specs=VMEM,
        compiler_params=pltpu.CompilerParams(vmem_limit_bytes=32 * 1024 * 1024),
        cost_estimate=pl.CostEstimate(flops=1_200_000_000, bytes_accessed=1_600_000, transcendentals=0),
    )(block, edge, sources)


def swap_axes(value):
    return lax.ppermute(value, ("c", "zl"), [(0, 0), (1, 2), (2, 1), (3, 3)])


def from_other_core(parts):
    return [lax.ppermute(p, "c", ring(2, 1)) for p in parts]


def per_device(sequence, conv_weight, conv_bias, norm_gain, proj_weight, out_weight, cotangent):
    zh, y, c, zl, x = (lax.axis_index(a) for a in ("zh", "y", "c", "zl", "x"))
    zring = ("zh", "zl")
    pos = jnp.stack([c, x, y, zh * 2 + zl])

    edge = jnp.where(zl == 0, sequence[0, -HALO:], sequence[0, :HALO])
    edge = lax.ppermute(edge, "zl", ring(2, 1))
    block = order_lanes(sequence[0], edge, lane_sources(zh, y, c, zl)[None])

    split = conv_weight.reshape(11, KW, NX, OUTC).transpose(2, 1, 0, 3)
    mine = jnp.zeros((NX, KW, 11, OUTC), bf16)
    for k in range(NX):
        piece = lax.dynamic_index_in_dim(split, (x + k) % NX, 0, keepdims=False)
        if k:
            piece = lax.ppermute(piece, "x", ring(NX, k))
        mine = lax.dynamic_update_index_in_dim(mine, piece, (x + NX - k) % NX, 0)
    mine = mine.transpose(1, 0, 2, 3).reshape(KW, GROUP, OUTC)
    mine = jnp.pad(mine, ((0, 0), (0, SLOT - GROUP), (0, 0)))

    later = jnp.concatenate([proj_weight.reshape(96, 3 * HD), out_weight.T], axis=1).reshape(48, D)
    later = swap_axes(jnp.concatenate([cotangent[0], later], axis=0))

    head_w = lax.all_gather(later[128:].reshape(96, 768), "y", axis=0)

    ypieces = [mine] + [lax.ppermute(mine, "y", ring(4, k)) for k in (1, 2, 3)]
    *ypieces, block = lax.optimization_barrier((*ypieces, block))
    ypieces = jnp.stack(ypieces)
    zpieces = [lax.ppermute(ypieces, zring, ring(4, k)) for k in (1, -1, 2)]
    xlow, xhigh = (lax.ppermute(block, "x", ring(4, k)) for k in (1, -1))
    yother = lax.ppermute(ypieces, "c", ring(2, 1))
    zpieces[0], xlow, xhigh, yother = lax.optimization_barrier((zpieces[0], xlow, xhigh, yother))
    xfar = across(xlow, xhigh, "x", 128)
    zothers = from_other_core(zpieces[:2])
    *zpieces, xa, xb, za, zb, head_w, cot = lax.optimization_barrier((*zpieces, *xfar, *zothers, head_w, later[:128]))
    cot = lax.all_gather(cot, ("c", "x"), axis=0, tiled=True)
    xpieces = [block, xlow, xhigh, xa, xb]
    wpieces = [ypieces, *zpieces, yother, za, zb, *from_other_core(zpieces[2:])]
    head_w = [head_w, *staged_ring(head_w, zring, 2)]
    bias = lax.dynamic_slice_in_dim(conv_bias, x * OUTC, OUTC)[None]

    feat = swap_axes(conv_pool(pos, xpieces, wpieces, bias))
    feats = [feat, *staged_ring(feat, "x", 256)]
    feats = feats + from_other_core(feats)

    normed, qkv, mixed, partial, own, wo = forward(pos, feats, norm_gain[None], head_w)
    attended = lax.psum_scatter(partial, ("c", "x"), scatter_dimension=0, tiled=True)
    block_out = (own.astype(f32) + attended.astype(f32)).astype(bf16)
    parts = lax.all_to_all(backward(qkv, cot, wo, normed, mixed), ("zh", "y", "zl"), 0, 0)
    parts, block_out = lax.optimization_barrier((parts, block_out))

    sums = total_parts(parts)
    rows = lax.ppermute(sums[:, 3 * HD :], ("zh", "c", "zl"), [(0, 4), (1, 6), (2, 5), (3, 7), (4, 0), (5, 2), (6, 1), (7, 3)])
    sums, rows, block_out = lax.optimization_barrier((swap_axes(sums), rows, swap_axes(block_out)))
    rows = jnp.stack([sums[:, 3 * HD :], rows])
    rows = jnp.stack([rows] + [lax.ppermute(rows, "y", ring(4, k)) for k in (1, 2, 3)])
    heads = lax.all_to_all(jnp.broadcast_to(sums[None, :, : 3 * HD], (8, 96, 3 * HD)), ("zl", "x"), 0, 0)
    proj_grad = place_proj(heads).transpose(1, 0, 2)
    out_grad = place_out(pos, rows, lax.ppermute(rows, "c", ring(2, 1)))
    return (block_out[None], proj_grad, out_grad)


def solution(mesh):
    fine = Mesh(mesh.devices.reshape(2, 4, 2, 2, 4), ("zh", "y", "c", "zl", "x"))
    dp, seq = ("zh", "y", "c"), ("zl", "x")
    in_specs = (
        P(dp, seq, None),
        P(dp + seq, None, None),
        P(),
        P(),
        P(dp, None, seq),
        P(seq, dp),
        P(dp, seq, None),
    )
    out_specs = (P(dp, seq, None), P(dp, None, None), P(seq, None))
    return jax.shard_map(per_device, mesh=fine, in_specs=in_specs, out_specs=out_specs, check_vma=False)
```

```python
import jax
import jax.numpy as jnp
import numpy as np
from jax import lax
from jax.experimental import pallas as pl
from jax.experimental.pallas import tpu as pltpu
from jax.sharding import Mesh, PartitionSpec as P

HD = 192
D = 1536
NX = 4
CIN = 1408
GROUP = 44
SLOT = 48
PLANE = 32
KPAD = PLANE * SLOT
OUTC = D // NX
KW = 5
EPS = 1e-06
HALO = 16
ROWS = 1024

bf16 = jnp.bfloat16
f32 = jnp.float32


def ring(n, k):
    return [(i, (i + k) % n) for i in range(n)]


def across(low, high, axis, cut):
    far_a = lax.ppermute(lax.slice_in_dim(low, 0, cut), axis, ring(4, 1))
    far_b = lax.ppermute(lax.slice_in_dim(high, cut, None), axis, ring(4, -1))
    return far_a, far_b


def staged_ring(block, axis, cut):
    low = lax.ppermute(block, axis, ring(4, 1))
    high = lax.ppermute(block, axis, ring(4, -1))
    return low, high, *across(low, high, axis, cut)


def conv_kernel(pos_ref, *refs):
    (x0, x1, x2, x3a, x3b, w0, w1, w2, w3, o0, o1, o2, o3, bias_ref, out_ref, wcat, xs, *accs) = refs
    row = 0
    for ref in (w0, w1, w2, w3, o0, o1, o2, o3):
        for piece in range(ref.shape[0]):
            for off in range(KW):
                wcat[row : row + SLOT, off * OUTC : (off + 1) * OUTC] = ref[piece, off]
            row += SLOT
    x, half = pos_ref[1], pos_ref[3] % 2
    zeros = jnp.zeros((HALO, KPAD), bf16)
    xs[0:HALO, :] = zeros
    xs[HALO + 1024 : 2 * HALO + 1024, :] = zeros

    def place_halo(b, edge):
        @pl.when(jnp.logical_and(half == 0, b == 0))
        def _():
            xs[HALO + 1024 : 2 * HALO + 1024, :] = edge()

        @pl.when(jnp.logical_and(half == 1, b == 3))
        def _():
            xs[0:HALO, :] = edge()

    for ref, step in ((x0, 0), (x1, 3), (x2, 1)):
        b = (x + step) % NX
        xs[pl.ds(pl.multiple_of(HALO + b * 256, HALO), 256), :] = ref[0:256, :]
        place_halo(b, lambda ref=ref: ref[256 : 256 + HALO, :])
    b = (x + 2) % NX
    xs[pl.ds(pl.multiple_of(HALO + b * 256, HALO), 128), :] = x3a[...]
    xs[pl.ds(pl.multiple_of(HALO + b * 256 + 128, HALO), 128), :] = x3b[0:128, :]
    place_halo(b, lambda: x3b[128 : 128 + HALO, :])

    @pl.loop(0, 1024 // ROWS)
    def _(r):
        base = pl.multiple_of(r * ROWS, ROWS)
        y = jnp.dot(xs[pl.ds(base, ROWS + 2 * HALO), :], wcat[...], preferred_element_type=f32)
        total = bias_ref[...] + jnp.zeros((ROWS, OUTC), f32)
        for off in range(KW):
            first = HALO + off - 2
            total = total + y[first : first + ROWS, off * OUTC : (off + 1) * OUTC]
        activated = jax.nn.gelu(total)
        for n, acc in enumerate(accs):
            acc[...] = activated[:, n * 128 : (n + 1) * 128]
            top = jnp.maximum(acc[pl.ds(0, ROWS // 2, 2), :], acc[pl.ds(1, ROWS // 2, 2), :])
            out_ref[pl.ds(pl.multiple_of(r * (ROWS // 2), ROWS // 2), ROWS // 2), n * 128 : (n + 1) * 128] = top.astype(bf16)


VMEM = pl.BlockSpec(memory_space=pltpu.VMEM)
SMEM = pl.BlockSpec(memory_space=pltpu.SMEM)


def conv_pool(pos, xpieces, wpieces, bias):
    return pl.pallas_call(
        conv_kernel,
        out_shape=jax.ShapeDtypeStruct((512, OUTC), bf16),
        in_specs=[SMEM] + [VMEM] * (len(xpieces) + len(wpieces) + 1),
        out_specs=VMEM,
        scratch_shapes=[
            pltpu.VMEM((KPAD, KW * OUTC), bf16),
            pltpu.VMEM((1024 + 2 * HALO, KPAD), bf16),
            *[pltpu.VMEM((ROWS, 128), f32)] * 3,
        ],
        compiler_params=pltpu.CompilerParams(vmem_limit_bytes=48 * 1024 * 1024),
        cost_estimate=pl.CostEstimate(flops=6_000_000_000, bytes_accessed=9_000_000, transcendentals=400_000),
    )(pos, *xpieces, *wpieces, bias)


SCALE = HD ** (-0.5)
WIDE = 256
TOKENS = 1024
BLOCK = 512
NT = (((1,), (1,)), ((), ()))
TN = (((0,), (0,)), ((), ()))


def dot(a, b, dims=(((1,), (0,)), ((), ()))):
    return lax.dot_general(a, b, dims, preferred_element_type=f32)


def softmax_rows(q_block, keys):
    scores = dot(q_block, keys, NT) * SCALE
    exponent = jnp.exp(scores - jnp.max(scores, axis=-1, keepdims=True))
    return exponent * (1.0 / jnp.sum(exponent, axis=-1, keepdims=True))


def forward_kernel(pos_ref, *refs):
    feat_refs, refs = refs[:10], refs[10:]
    (gain_ref, z0, z1, z2, z3a, z3b, normed_ref, qkv_ref, mixed_ref, partial_ref, own_ref, wo, feats, wq) = refs
    c, x, z = pos_ref[0], pos_ref[1], pos_ref[3]
    for t in range(3):
        wq[:, t * WIDE + HD : (t + 1) * WIDE] = jnp.zeros((D, WIDE - HD), bf16)
    wo[:, HD:] = jnp.zeros((D, WIDE - HD), bf16)
    for ref, zstep, first in ((z0, 0, 0), (z1, 3, 0), (z2, 1, 0), (z3a, 2, 0), (z3b, 2, 2)):
        for k in range(ref.shape[0]):
            src_z, src_y = (z + zstep) % 4, first + k
            rows = pl.ds(pl.multiple_of((((src_z // 2) * 4 + src_y) * 2 + src_z % 2) * 96, 96), 96)
            piece = ref[k]
            for t in range(3):
                wq[rows, t * WIDE : t * WIDE + HD] = piece[:, t * HD : (t + 1) * HD]
            wo[rows, :HD] = piece[:, 3 * HD :]

    for side in range(2):
        half = c if side == 0 else 1 - c
        for ref, step, first in zip(feat_refs[side * 5 : side * 5 + 5], (0, 3, 1, 2, 2), (0, 0, 0, 0, 256)):
            size = ref.shape[0]
            rows = pl.ds(pl.multiple_of(half * 512 + first, 256), size)
            lanes = pl.ds(pl.multiple_of(((x + step) % NX) * OUTC, 128), OUTC)
            feats[rows, lanes] = ref[...]
    own_ref[...] = feats[pl.ds(pl.multiple_of((c * NX + x) * 128, 128), 128), :]

    @pl.loop(0, TOKENS // BLOCK)
    def _(r):
        rows = pl.ds(pl.multiple_of(r * BLOCK, BLOCK), BLOCK)
        part = feats[rows, :].astype(f32)
        factor = lax.rsqrt(jnp.sum(part * part, axis=-1, keepdims=True) * (1.0 / D) + EPS)
        normed = (part * factor * gain_ref[...]).astype(bf16)
        normed_ref[rows, :] = normed
        qkv = dot(normed, wq[...]).astype(bf16)
        for t in range(3):
            qkv_ref[t, rows, :] = qkv[:, t * WIDE : (t + 1) * WIDE]

    @pl.loop(0, TOKENS // BLOCK)
    def _(r):
        rows = pl.ds(pl.multiple_of(r * BLOCK, BLOCK), BLOCK)
        weights = softmax_rows(qkv_ref[0, rows, :], qkv_ref[1]).astype(bf16)
        mixed = dot(weights, qkv_ref[2]).astype(bf16)
        mixed_ref[rows, :] = mixed
        partial_ref[rows, :] = dot(mixed, wo[...], NT).astype(bf16)


def forward(pos, feats, gain, wpieces):
    return pl.pallas_call(
        forward_kernel,
        out_shape=(
            jax.ShapeDtypeStruct((TOKENS, D), bf16),
            jax.ShapeDtypeStruct((3, TOKENS, WIDE), bf16),
            jax.ShapeDtypeStruct((TOKENS, WIDE), bf16),
            jax.ShapeDtypeStruct((TOKENS, D), bf16),
            jax.ShapeDtypeStruct((128, D), bf16),
            jax.ShapeDtypeStruct((D, WIDE), bf16),
        ),
        in_specs=[SMEM] + [VMEM] * 16,
        out_specs=[VMEM] * 6,
        scratch_shapes=[pltpu.VMEM((TOKENS, D), bf16), pltpu.VMEM((D, 3 * WIDE), bf16)],
        compiler_params=pltpu.CompilerParams(vmem_limit_bytes=48 * 1024 * 1024),
        cost_estimate=pl.CostEstimate(flops=4_000_000_000, bytes_accessed=16_000_000, transcendentals=1_100_000),
    )(pos, *feats, gain, *wpieces)


def backward_kernel(
    qkv_ref, cot_ref, wo, normed_ref, mixed_ref, sent_ref, dcat, dk, dv, grads, outs
):
    @pl.loop(0, TOKENS // BLOCK)
    def _(r):
        rows = pl.ds(pl.multiple_of(r * BLOCK, BLOCK), BLOCK)
        d_mixed = dot(cot_ref[rows, :], wo[...]).astype(bf16)
        q_block = qkv_ref[0, rows, :]
        weights = softmax_rows(q_block, qkv_ref[1])
        d_weights = dot(d_mixed, qkv_ref[2], NT)
        centre = jnp.sum(weights * d_weights, axis=-1, keepdims=True)
        d_scores = (weights * (d_weights - centre) * SCALE).astype(bf16)
        dcat[rows, 0:HD] = dot(d_scores, qkv_ref[1]).astype(bf16)[:, :HD]
        d_value = dot(d_mixed, weights.astype(bf16), TN)
        d_key = dot(q_block, d_scores, TN)

        @pl.when(r == 0)
        def _():
            dv[...] = d_value
            dk[...] = d_key

        @pl.when(r > 0)
        def _():
            dv[...] += d_value
            dk[...] += d_key

    dcat[:, HD : 2 * HD] = dk[...].T.astype(bf16)[:, :HD]
    dcat[:, 2 * HD : 3 * HD] = dv[...].T.astype(bf16)[:, :HD]

    @pl.loop(0, 4)
    def _(n):
        lanes = pl.ds(pl.multiple_of(n * 384, 384), 384)
        grads[lanes, :] = dot(normed_ref[:, lanes], dcat[...], TN)
        outs[:, lanes] = dot(mixed_ref[...], cot_ref[:, lanes], TN)[:HD]

    for d in range(16):
        sent_ref[d, :, : 3 * HD] = grads[d * 96 : (d + 1) * 96, :].astype(bf16)
        g, lane = d // 2, (d % 2) * 768
        packed = [outs[g * 24 : (g + 1) * 24, lane + j * HD : lane + (j + 1) * HD] for j in range(4)]
        sent_ref[d, :, 3 * HD :] = jnp.concatenate(packed, axis=0).astype(bf16)


def backward(qkv, cot, wo, normed, mixed):
    return pl.pallas_call(
        backward_kernel,
        out_shape=jax.ShapeDtypeStruct((16, 96, 768), bf16),
        in_specs=[VMEM] * 5,
        out_specs=VMEM,
        scratch_shapes=[
            pltpu.VMEM((TOKENS, 3 * HD), bf16),
            pltpu.VMEM((WIDE, TOKENS), f32),
            pltpu.VMEM((WIDE, TOKENS), f32),
            pltpu.VMEM((D, 3 * HD), f32),
            pltpu.VMEM((HD, D), f32),
        ],
        compiler_params=pltpu.CompilerParams(vmem_limit_bytes=56 * 1024 * 1024),
        cost_estimate=pl.CostEstimate(flops=6_000_000_000, bytes_accessed=18_000_000, transcendentals=1_100_000),
    )(qkv, cot, wo, normed, mixed)


def total_kernel(parts_ref, out_ref, rows_ref):
    total = parts_ref[0].astype(f32)
    for g in range(1, 16):
        total = total + parts_ref[g].astype(f32)
    out_ref[...] = total.astype(bf16)
    rows_ref[...] = total[:, 3 * HD :].astype(bf16)


def total_parts(parts):
    return pl.pallas_call(
        total_kernel,
        out_shape=(jax.ShapeDtypeStruct((96, 768), bf16), jax.ShapeDtypeStruct((96, HD), bf16)),
        in_specs=[VMEM],
        out_specs=[VMEM] * 2,
    )(parts)


def proj_kernel(heads_ref, out_ref):
    for h in range(8):
        for t in range(3):
            out_ref[t, :, h * HD : (h + 1) * HD] = heads_ref[h, :, t * HD : (t + 1) * HD].astype(f32)


def place_proj(heads):
    return pl.pallas_call(
        proj_kernel,
        out_shape=jax.ShapeDtypeStruct((3, 96, D), f32),
        in_specs=[VMEM],
        out_specs=VMEM,
    )(heads)


def out_kernel(pos_ref, own_ref, other_ref, out_ref):
    c, y, zh = pos_ref[0], pos_ref[2], pos_ref[3] // 2
    for ref, core in ((own_ref, c), (other_ref, 1 - c)):
        lanes = pl.ds(pl.multiple_of(core * 768, 768), 768)
        for step in range(2):
            for k in range(4):
                g = ((zh + step) % 2) * 4 + (y + 4 - k) % 4
                piece = [ref[k, step, j * 24 : (j + 1) * 24, :] for j in range(4)]
                rows = pl.ds(pl.multiple_of(g * 24, 8), 24)
                out_ref[rows, lanes] = jnp.concatenate(piece, axis=1).astype(f32)


def place_out(pos, own, other):
    return pl.pallas_call(
        out_kernel,
        out_shape=jax.ShapeDtypeStruct((HD, D), f32),
        in_specs=[SMEM, VMEM, VMEM],
        out_specs=VMEM,
    )(pos, own, other)


def lane_sources(zh, y, c, zl):
    lane = lax.iota(jnp.int32, KPAD)
    slot, j = lane // SLOT, lane % SLOT
    core = jnp.where(slot < 16, c, 1 - c)
    within = slot % 16
    zstep = within // 4
    ystep = within % 4
    z = zh * 2 + zl
    src_z = (z + jnp.where(zstep == 1, 3, jnp.where(zstep == 2, 1, jnp.where(zstep == 3, 2, 0)))) % 4
    src_y = (y + 4 - ystep) % 4
    plane = (((src_z // 2) * 4 + src_y) * 2 + core) * 2 + src_z % 2
    return jnp.where(j < GROUP, plane * GROUP + j, -1)


def lanes_kernel(block_ref, edge_ref, sources_ref, out_ref):
    for n in range(4):
        lanes = slice(n * 384, (n + 1) * 384)
        select = lax.broadcasted_iota(jnp.int32, (CIN, 384), 0) == sources_ref[:, lanes]
        select = jnp.where(select, 1.0, 0.0).astype(bf16)
        out_ref[0:256, lanes] = dot(block_ref[...], select).astype(bf16)
        out_ref[256:, lanes] = dot(edge_ref[...], select).astype(bf16)


def order_lanes(block, edge, sources):
    return pl.pallas_call(
        lanes_kernel,
        out_shape=jax.ShapeDtypeStruct((256 + HALO, KPAD), bf16),
        in_specs=[VMEM] * 3,
        out_specs=VMEM,
        compiler_params=pltpu.CompilerParams(vmem_limit_bytes=32 * 1024 * 1024),
        cost_estimate=pl.CostEstimate(flops=1_200_000_000, bytes_accessed=1_600_000, transcendentals=0),
    )(block, edge, sources)


def swap_axes(value):
    return lax.ppermute(value, ("c", "zl"), [(0, 0), (1, 2), (2, 1), (3, 3)])


def from_other_core(parts):
    return [lax.ppermute(p, "c", ring(2, 1)) for p in parts]


def per_device(sequence, conv_weight, conv_bias, norm_gain, proj_weight, out_weight, cotangent):
    zh, y, c, zl, x = (lax.axis_index(a) for a in ("zh", "y", "c", "zl", "x"))
    zring = ("zh", "zl")
    pos = jnp.stack([c, x, y, zh * 2 + zl])

    edge = jnp.where(zl == 0, sequence[0, -HALO:], sequence[0, :HALO])
    edge = lax.ppermute(edge, "zl", ring(2, 1))
    block = order_lanes(sequence[0], edge, lane_sources(zh, y, c, zl)[None])

    split = conv_weight.reshape(11, KW, NX, OUTC).transpose(2, 1, 0, 3)
    mine = jnp.zeros((NX, KW, 11, OUTC), bf16)
    for k in range(NX):
        piece = lax.dynamic_index_in_dim(split, (x + k) % NX, 0, keepdims=False)
        if k:
            piece = lax.ppermute(piece, "x", ring(NX, k))
        mine = lax.dynamic_update_index_in_dim(mine, piece, (x + NX - k) % NX, 0)
    mine = mine.transpose(1, 0, 2, 3).reshape(KW, GROUP, OUTC)
    mine = jnp.pad(mine, ((0, 0), (0, SLOT - GROUP), (0, 0)))

    later = jnp.concatenate([proj_weight.reshape(96, 3 * HD), out_weight.T], axis=1).reshape(48, D)
    later = swap_axes(jnp.concatenate([cotangent[0], later], axis=0))

    head_w = lax.all_gather(later[128:].reshape(96, 768), "y", axis=0)

    ypieces = [mine] + [lax.ppermute(mine, "y", ring(4, k)) for k in (1, 2, 3)]
    *ypieces, block = lax.optimization_barrier((*ypieces, block))
    ypieces = jnp.stack(ypieces)
    zpieces = [lax.ppermute(ypieces, zring, ring(4, k)) for k in (1, -1, 2)]
    xlow, xhigh = (lax.ppermute(block, "x", ring(4, k)) for k in (1, -1))
    yother = lax.ppermute(ypieces, "c", ring(2, 1))
    zpieces[0], xlow, xhigh, yother = lax.optimization_barrier((zpieces[0], xlow, xhigh, yother))
    xfar = across(xlow, xhigh, "x", 128)
    zothers = from_other_core(zpieces[:2])
    *zpieces, xa, xb, za, zb, head_w, cot = lax.optimization_barrier((*zpieces, *xfar, *zothers, head_w, later[:128]))
    cot = lax.all_gather(cot, ("c", "x"), axis=0, tiled=True)
    xpieces = [block, xlow, xhigh, xa, xb]
    wpieces = [ypieces, *zpieces, yother, za, zb, *from_other_core(zpieces[2:])]
    head_w = [head_w, *staged_ring(head_w, zring, 2)]
    bias = lax.dynamic_slice_in_dim(conv_bias, x * OUTC, OUTC)[None]

    feat = swap_axes(conv_pool(pos, xpieces, wpieces, bias))
    feats = [feat, *staged_ring(feat, "x", 256)]
    feats = feats + from_other_core(feats)

    normed, qkv, mixed, partial, own, wo = forward(pos, feats, norm_gain[None], head_w)
    attended = lax.psum_scatter(partial, ("c", "x"), scatter_dimension=0, tiled=True)
    block_out = (own.astype(f32) + attended.astype(f32)).astype(bf16)
    parts = lax.all_to_all(backward(qkv, cot, wo, normed, mixed), ("zh", "y", "zl"), 0, 0)
    sums, rows = total_parts(parts)
    rows = lax.ppermute(rows, ("zh", "c", "zl"), [(0, 4), (1, 6), (2, 5), (3, 7), (4, 0), (5, 2), (6, 1), (7, 3)])
    sums, rows, block_out = lax.optimization_barrier((swap_axes(sums), rows, block_out))
    block_out = swap_axes(block_out)
    rows = jnp.stack([sums[:, 3 * HD :], rows])
    rows = jnp.stack([rows] + [lax.ppermute(rows, "y", ring(4, k)) for k in (1, 2, 3)])
    heads = lax.all_to_all(jnp.broadcast_to(sums[None, :, : 3 * HD], (8, 96, 3 * HD)), ("zl", "x"), 0, 0)
    out_grad = place_out(pos, rows, lax.ppermute(rows, "c", ring(2, 1)))
    proj_grad, block_out = lax.optimization_barrier((place_proj(heads), block_out))
    proj_grad = proj_grad.transpose(1, 0, 2)
    return (block_out[None], proj_grad, out_grad)


def solution(mesh):
    fine = Mesh(mesh.devices.reshape(2, 4, 2, 2, 4), ("zh", "y", "c", "zl", "x"))
    dp, seq = ("zh", "y", "c"), ("zl", "x")
    in_specs = (
        P(dp, seq, None),
        P(dp + seq, None, None),
        P(),
        P(),
        P(dp, None, seq),
        P(seq, dp),
        P(dp, seq, None),
    )
    out_specs = (P(dp, seq, None), P(dp, None, None), P(seq, None))
    return jax.shard_map(per_device, mesh=fine, in_specs=in_specs, out_specs=out_specs, check_vma=False)
```

```python
import jax
import jax.numpy as jnp
import numpy as np
from jax import lax
from jax.experimental import pallas as pl
from jax.experimental.pallas import tpu as pltpu
from jax.sharding import Mesh, PartitionSpec as P

HD = 192
D = 1536
NX = 4
CIN = 1408
GROUP = 44
SLOT = 48
PLANE = 32
KPAD = PLANE * SLOT
OUTC = D // NX
KW = 5
EPS = 1e-06
HALO = 16
ROWS = 1024

bf16 = jnp.bfloat16
f32 = jnp.float32


def ring(n, k):
    return [(i, (i + k) % n) for i in range(n)]


def across(low, high, axis, cut):
    far_a = lax.ppermute(lax.slice_in_dim(low, 0, cut), axis, ring(4, 1))
    far_b = lax.ppermute(lax.slice_in_dim(high, cut, None), axis, ring(4, -1))
    return far_a, far_b


def staged_ring(block, axis, cut):
    low = lax.ppermute(block, axis, ring(4, 1))
    high = lax.ppermute(block, axis, ring(4, -1))
    return low, high, *across(low, high, axis, cut)


def conv_kernel(pos_ref, *refs):
    (x0, x1, x2, x3a, x3b, w0, w1, w2, w3, o0, o1, o2, o3, bias_ref, out_ref, wcat, xs, *accs) = refs
    row = 0
    for ref in (w0, w1, w2, w3, o0, o1, o2, o3):
        for piece in range(ref.shape[0]):
            for off in range(KW):
                wcat[row : row + SLOT, off * OUTC : (off + 1) * OUTC] = ref[piece, off]
            row += SLOT
    x, half = pos_ref[1], pos_ref[3] % 2
    zeros = jnp.zeros((HALO, KPAD), bf16)
    xs[0:HALO, :] = zeros
    xs[HALO + 1024 : 2 * HALO + 1024, :] = zeros

    def place_halo(b, edge):
        @pl.when(jnp.logical_and(half == 0, b == 0))
        def _():
            xs[HALO + 1024 : 2 * HALO + 1024, :] = edge()

        @pl.when(jnp.logical_and(half == 1, b == 3))
        def _():
            xs[0:HALO, :] = edge()

    for ref, step in ((x0, 0), (x1, 3), (x2, 1)):
        b = (x + step) % NX
        xs[pl.ds(pl.multiple_of(HALO + b * 256, HALO), 256), :] = ref[0:256, :]
        place_halo(b, lambda ref=ref: ref[256 : 256 + HALO, :])
    b = (x + 2) % NX
    xs[pl.ds(pl.multiple_of(HALO + b * 256, HALO), 128), :] = x3a[...]
    xs[pl.ds(pl.multiple_of(HALO + b * 256 + 128, HALO), 128), :] = x3b[0:128, :]
    place_halo(b, lambda: x3b[128 : 128 + HALO, :])

    @pl.loop(0, 1024 // ROWS)
    def _(r):
        base = pl.multiple_of(r * ROWS, ROWS)
        y = jnp.dot(xs[pl.ds(base, ROWS + 2 * HALO), :], wcat[...], preferred_element_type=f32)
        total = bias_ref[...] + jnp.zeros((ROWS, OUTC), f32)
        for off in range(KW):
            first = HALO + off - 2
            total = total + y[first : first + ROWS, off * OUTC : (off + 1) * OUTC]
        activated = jax.nn.gelu(total)
        for n, acc in enumerate(accs):
            acc[...] = activated[:, n * 128 : (n + 1) * 128]
            top = jnp.maximum(acc[pl.ds(0, ROWS // 2, 2), :], acc[pl.ds(1, ROWS // 2, 2), :])
            out_ref[pl.ds(pl.multiple_of(r * (ROWS // 2), ROWS // 2), ROWS // 2), n * 128 : (n + 1) * 128] = top.astype(bf16)


VMEM = pl.BlockSpec(memory_space=pltpu.VMEM)
SMEM = pl.BlockSpec(memory_space=pltpu.SMEM)
ANY = pl.BlockSpec(memory_space=pl.ANY)


def conv_pool(pos, xpieces, wpieces, bias):
    return pl.pallas_call(
        conv_kernel,
        out_shape=jax.ShapeDtypeStruct((512, OUTC), bf16),
        in_specs=[SMEM] + [VMEM] * (len(xpieces) + len(wpieces) + 1),
        out_specs=VMEM,
        scratch_shapes=[
            pltpu.VMEM((KPAD, KW * OUTC), bf16),
            pltpu.VMEM((1024 + 2 * HALO, KPAD), bf16),
            *[pltpu.VMEM((ROWS, 128), f32)] * 3,
        ],
        compiler_params=pltpu.CompilerParams(vmem_limit_bytes=48 * 1024 * 1024),
        cost_estimate=pl.CostEstimate(flops=6_000_000_000, bytes_accessed=9_000_000, transcendentals=400_000),
    )(pos, *xpieces, *wpieces, bias)


SCALE = HD ** (-0.5)
WIDE = 256
TOKENS = 1024
BLOCK = 1024
NT = (((1,), (1,)), ((), ()))
TN = (((0,), (0,)), ((), ()))


def dot(a, b, dims=(((1,), (0,)), ((), ()))):
    return lax.dot_general(a, b, dims, preferred_element_type=f32)


def softmax_rows(q_block, keys):
    scores = dot(q_block, keys, NT) * SCALE
    exponent = jnp.exp(scores - jnp.max(scores, axis=-1, keepdims=True))
    return exponent * (1.0 / jnp.sum(exponent, axis=-1, keepdims=True))


def forward_kernel(pos_ref, *refs):
    feat_refs, refs = refs[:10], refs[10:]
    (gain_ref, z0, z1, z2, z3a, z3b, normed_out, qkv_out, mixed_ref, partial_out, own_ref, wo_out) = refs[:12]
    (normed_ref, qkv_ref, partial_ref, wo, feats, wq, sems) = refs[12:]
    c, x, z = pos_ref[0], pos_ref[1], pos_ref[3]
    for t in range(3):
        wq[:, t * WIDE + HD : (t + 1) * WIDE] = jnp.zeros((D, WIDE - HD), bf16)
    wo[:, HD:] = jnp.zeros((D, WIDE - HD), bf16)
    for ref, zstep, first in ((z0, 0, 0), (z1, 3, 0), (z2, 1, 0), (z3a, 2, 0), (z3b, 2, 2)):
        for k in range(ref.shape[0]):
            src_z, src_y = (z + zstep) % 4, first + k
            rows = pl.ds(pl.multiple_of((((src_z // 2) * 4 + src_y) * 2 + src_z % 2) * 96, 96), 96)
            piece = ref[k]
            for t in range(3):
                wq[rows, t * WIDE : t * WIDE + HD] = piece[:, t * HD : (t + 1) * HD]
            wo[rows, :HD] = piece[:, 3 * HD :]

    for side in range(2):
        half = c if side == 0 else 1 - c
        for ref, step, first in zip(feat_refs[side * 5 : side * 5 + 5], (0, 3, 1, 2, 2), (0, 0, 0, 0, 256)):
            size = ref.shape[0]
            rows = pl.ds(pl.multiple_of(half * 512 + first, 256), size)
            lanes = pl.ds(pl.multiple_of(((x + step) % NX) * OUTC, 128), OUTC)
            feats[rows, lanes] = ref[...]
    own_ref[...] = feats[pl.ds(pl.multiple_of((c * NX + x) * 128, 128), 128), :]

    @pl.loop(0, TOKENS // BLOCK)
    def _(r):
        rows = pl.ds(pl.multiple_of(r * BLOCK, BLOCK), BLOCK)
        part = feats[rows, :].astype(f32)
        factor = lax.rsqrt(jnp.sum(part * part, axis=-1, keepdims=True) * (1.0 / D) + EPS)
        normed = (part * factor * gain_ref[...]).astype(bf16)
        normed_ref[rows, :] = normed
        qkv = dot(normed, wq[...]).astype(bf16)
        for t in range(3):
            qkv_ref[t, rows, :] = qkv[:, t * WIDE : (t + 1) * WIDE]

    early = [
        pltpu.make_async_copy(source, target, sems.at[n])
        for n, (source, target) in enumerate(((normed_ref, normed_out), (qkv_ref, qkv_out), (wo, wo_out)))
    ]
    for copy in early:
        copy.start()
    late = []
    for r in range(TOKENS // BLOCK):
        rows = slice(r * BLOCK, (r + 1) * BLOCK)
        weights = softmax_rows(qkv_ref[0, rows, :], qkv_ref[1]).astype(bf16)
        mixed = dot(weights, qkv_ref[2]).astype(bf16)
        mixed_ref[rows, :] = mixed
        partial_ref[rows, :] = dot(mixed, wo[...], NT).astype(bf16)
        late.append(pltpu.make_async_copy(partial_ref.at[pl.ds(r * BLOCK, BLOCK)], partial_out.at[pl.ds(r * BLOCK, BLOCK)], sems.at[3 + r]))
        late[-1].start()
    for copy in early + late:
        copy.wait()


def forward(pos, feats, gain, wpieces):
    return pl.pallas_call(
        forward_kernel,
        out_shape=(
            jax.ShapeDtypeStruct((TOKENS, D), bf16),
            jax.ShapeDtypeStruct((3, TOKENS, WIDE), bf16),
            jax.ShapeDtypeStruct((TOKENS, WIDE), bf16),
            jax.ShapeDtypeStruct((TOKENS, D), bf16),
            jax.ShapeDtypeStruct((128, D), bf16),
            jax.ShapeDtypeStruct((D, WIDE), bf16),
        ),
        in_specs=[SMEM] + [VMEM] * 16,
        out_specs=[ANY, ANY, VMEM, ANY, VMEM, ANY],
        scratch_shapes=[
            pltpu.VMEM((TOKENS, D), bf16),
            pltpu.VMEM((3, TOKENS, WIDE), bf16),
            pltpu.VMEM((TOKENS, D), bf16),
            pltpu.VMEM((D, WIDE), bf16),
            pltpu.VMEM((TOKENS, D), bf16),
            pltpu.VMEM((D, 3 * WIDE), bf16),
            pltpu.SemaphoreType.DMA((3 + TOKENS // BLOCK,)),
        ],
        compiler_params=pltpu.CompilerParams(vmem_limit_bytes=48 * 1024 * 1024),
        cost_estimate=pl.CostEstimate(flops=4_000_000_000, bytes_accessed=16_000_000, transcendentals=1_100_000),
    )(pos, *feats, gain, *wpieces)


def backward_kernel(
    qkv_ref, cot_in, wo, normed_in, mixed_ref, sent_ref, cot_ref, normed_ref, dcat, dk, dv, grads, outs, sems
):
    cot_copy = pltpu.make_async_copy(cot_in, cot_ref, sems.at[0])
    normed_copy = pltpu.make_async_copy(normed_in, normed_ref, sems.at[1])
    cot_copy.start()
    normed_copy.start()

    for r in range(TOKENS // BLOCK):
        rows = slice(r * BLOCK, (r + 1) * BLOCK)
        q_block = qkv_ref[0, rows, :]
        weights = softmax_rows(q_block, qkv_ref[1])
        if r == 0:
            cot_copy.wait()
        d_mixed = dot(cot_ref[rows, :], wo[...]).astype(bf16)
        d_weights = dot(d_mixed, qkv_ref[2], NT)
        centre = jnp.sum(weights * d_weights, axis=-1, keepdims=True)
        d_scores = (weights * (d_weights - centre) * SCALE).astype(bf16)
        dcat[rows, 0:HD] = dot(d_scores, qkv_ref[1]).astype(bf16)[:, :HD]
        d_value = dot(d_mixed, weights.astype(bf16), TN)
        d_key = dot(q_block, d_scores, TN)
        dv[...] = d_value if r == 0 else dv[...] + d_value
        dk[...] = d_key if r == 0 else dk[...] + d_key
    normed_copy.wait()
    dcat[:, HD : 2 * HD] = dk[...].T.astype(bf16)[:, :HD]
    dcat[:, 2 * HD : 3 * HD] = dv[...].T.astype(bf16)[:, :HD]

    outs[...] = dot(mixed_ref[...], cot_ref[...], TN)[:HD]
    grads[...] = dot(normed_ref[...], dcat[...], TN)

    for d in range(16):
        sent_ref[d, :, : 3 * HD] = grads[d * 96 : (d + 1) * 96, :].astype(bf16)
        g, lane = d // 2, (d % 2) * 768
        packed = [outs[g * 24 : (g + 1) * 24, lane + j * HD : lane + (j + 1) * HD] for j in range(4)]
        sent_ref[d, :, 3 * HD :] = jnp.concatenate(packed, axis=0).astype(bf16)


def backward(qkv, cot, wo, normed, mixed):
    return pl.pallas_call(
        backward_kernel,
        out_shape=jax.ShapeDtypeStruct((16, 96, 768), bf16),
        in_specs=[VMEM, ANY, VMEM, ANY, VMEM],
        out_specs=VMEM,
        scratch_shapes=[
            pltpu.VMEM((TOKENS, D), bf16),
            pltpu.VMEM((TOKENS, D), bf16),
            pltpu.VMEM((TOKENS, 3 * HD), bf16),
            pltpu.VMEM((WIDE, TOKENS), f32),
            pltpu.VMEM((WIDE, TOKENS), f32),
            pltpu.VMEM((D, 3 * HD), f32),
            pltpu.VMEM((HD, D), f32),
            pltpu.SemaphoreType.DMA((2,)),
        ],
        compiler_params=pltpu.CompilerParams(vmem_limit_bytes=56 * 1024 * 1024),
        cost_estimate=pl.CostEstimate(flops=6_000_000_000, bytes_accessed=18_000_000, transcendentals=1_100_000),
    )(qkv, cot, wo, normed, mixed)


def total_kernel(parts_ref, out_ref, rows_ref):
    total = parts_ref[0].astype(f32)
    for g in range(1, 16):
        total = total + parts_ref[g].astype(f32)
    out_ref[...] = total.astype(bf16)
    rows_ref[...] = total[:, 3 * HD :].astype(bf16)


def total_parts(parts):
    return pl.pallas_call(
        total_kernel,
        out_shape=(jax.ShapeDtypeStruct((96, 768), bf16), jax.ShapeDtypeStruct((96, HD), bf16)),
        in_specs=[VMEM],
        out_specs=[VMEM] * 2,
    )(parts)


def proj_kernel(heads_in, out, heads, wide, sems):
    reads = [pltpu.make_async_copy(heads_in.at[h], heads.at[h], sems.at[h]) for h in range(8)]
    for copy in reads:
        copy.start()
    for h, copy in enumerate(reads):
        copy.wait()
        for t in range(3):
            wide[t, :, h * HD : (h + 1) * HD] = heads[h, :, t * HD : (t + 1) * HD].astype(f32)
    write = pltpu.make_async_copy(wide, out, sems.at[8])
    write.start()
    write.wait()


def place_proj(heads):
    return pl.pallas_call(
        proj_kernel,
        out_shape=jax.ShapeDtypeStruct((3, 96, D), f32),
        in_specs=[ANY],
        out_specs=ANY,
        scratch_shapes=[
            pltpu.VMEM((8, 96, 3 * HD), bf16),
            pltpu.VMEM((3, 96, D), f32),
            pltpu.SemaphoreType.DMA((9,)),
        ],
    )(heads)


def out_kernel(pos_ref, own_ref, other_ref, out_ref):
    c, y, zh = pos_ref[0], pos_ref[2], pos_ref[3] // 2
    for ref, core in ((own_ref, c), (other_ref, 1 - c)):
        lanes = pl.ds(pl.multiple_of(core * 768, 768), 768)
        for step in range(2):
            for k in range(4):
                g = ((zh + step) % 2) * 4 + (y + 4 - k) % 4
                piece = [ref[k, step, j * 24 : (j + 1) * 24, :] for j in range(4)]
                rows = pl.ds(pl.multiple_of(g * 24, 8), 24)
                out_ref[rows, lanes] = jnp.concatenate(piece, axis=1).astype(f32)


def place_out(pos, own, other):
    return pl.pallas_call(
        out_kernel,
        out_shape=jax.ShapeDtypeStruct((HD, D), f32),
        in_specs=[SMEM, VMEM, VMEM],
        out_specs=VMEM,
    )(pos, own, other)


def lane_sources(zh, y, c, zl):
    lane = lax.iota(jnp.int32, KPAD)
    slot, j = lane // SLOT, lane % SLOT
    core = jnp.where(slot < 16, c, 1 - c)
    within = slot % 16
    zstep = within // 4
    ystep = within % 4
    z = zh * 2 + zl
    src_z = (z + jnp.where(zstep == 1, 3, jnp.where(zstep == 2, 1, jnp.where(zstep == 3, 2, 0)))) % 4
    src_y = (y + 4 - ystep) % 4
    plane = (((src_z // 2) * 4 + src_y) * 2 + core) * 2 + src_z % 2
    return jnp.where(j < GROUP, plane * GROUP + j, -1)


def lanes_kernel(block_ref, edge_ref, sources_ref, out_ref):
    for n in range(4):
        lanes = slice(n * 384, (n + 1) * 384)
        select = lax.broadcasted_iota(jnp.int32, (CIN, 384), 0) == sources_ref[:, lanes]
        select = jnp.where(select, 1.0, 0.0).astype(bf16)
        out_ref[0:256, lanes] = dot(block_ref[...], select).astype(bf16)
        out_ref[256:, lanes] = dot(edge_ref[...], select).astype(bf16)


def order_lanes(block, edge, sources):
    return pl.pallas_call(
        lanes_kernel,
        out_shape=jax.ShapeDtypeStruct((256 + HALO, KPAD), bf16),
        in_specs=[VMEM] * 3,
        out_specs=VMEM,
        compiler_params=pltpu.CompilerParams(vmem_limit_bytes=32 * 1024 * 1024),
        cost_estimate=pl.CostEstimate(flops=1_200_000_000, bytes_accessed=1_600_000, transcendentals=0),
    )(block, edge, sources)


def swap_axes(value):
    return lax.ppermute(value, ("c", "zl"), [(0, 0), (1, 2), (2, 1), (3, 3)])


def from_other_core(parts):
    return [lax.ppermute(p, "c", ring(2, 1)) for p in parts]


def per_device(sequence, conv_weight, conv_bias, norm_gain, proj_weight, out_weight, cotangent):
    zh, y, c, zl, x = (lax.axis_index(a) for a in ("zh", "y", "c", "zl", "x"))
    zring = ("zh", "zl")
    pos = jnp.stack([c, x, y, zh * 2 + zl])

    edge = jnp.where(zl == 0, sequence[0, -HALO:], sequence[0, :HALO])
    edge = lax.ppermute(edge, "zl", ring(2, 1))
    block = order_lanes(sequence[0], edge, lane_sources(zh, y, c, zl)[None])

    split = conv_weight.reshape(11, KW, NX, OUTC).transpose(2, 1, 0, 3)
    mine = jnp.zeros((NX, KW, 11, OUTC), bf16)
    for k in range(NX):
        piece = lax.dynamic_index_in_dim(split, (x + k) % NX, 0, keepdims=False)
        if k:
            piece = lax.ppermute(piece, "x", ring(NX, k))
        mine = lax.dynamic_update_index_in_dim(mine, piece, (x + NX - k) % NX, 0)
    mine = mine.transpose(1, 0, 2, 3).reshape(KW, GROUP, OUTC)
    mine = jnp.pad(mine, ((0, 0), (0, SLOT - GROUP), (0, 0)))

    later = jnp.concatenate([proj_weight.reshape(96, 3 * HD), out_weight.T], axis=1).reshape(48, D)
    later = swap_axes(jnp.concatenate([cotangent[0], later], axis=0))

    head_w = lax.all_gather(later[128:].reshape(96, 768), "y", axis=0)

    ypieces = [mine] + [lax.ppermute(mine, "y", ring(4, k)) for k in (1, 2, 3)]
    *ypieces, block = lax.optimization_barrier((*ypieces, block))
    ypieces = jnp.stack(ypieces)
    zpieces = [lax.ppermute(ypieces, zring, ring(4, k)) for k in (1, -1, 2)]
    xlow, xhigh = (lax.ppermute(block, "x", ring(4, k)) for k in (1, -1))
    yother = lax.ppermute(ypieces, "c", ring(2, 1))
    zpieces[0], xlow, xhigh, yother = lax.optimization_barrier((zpieces[0], xlow, xhigh, yother))
    xfar = across(xlow, xhigh, "x", 128)
    zothers = from_other_core(zpieces[:2])
    *zpieces, xa, xb, za, zb, head_w, cot = lax.optimization_barrier((*zpieces, *xfar, *zothers, head_w, later[:128]))
    cot = lax.all_gather(cot, ("c", "x"), axis=0, tiled=True)
    xpieces = [block, xlow, xhigh, xa, xb]
    wpieces = [ypieces, *zpieces, yother, za, zb, *from_other_core(zpieces[2:])]
    head_w = [head_w, *staged_ring(head_w, zring, 2)]
    bias = lax.dynamic_slice_in_dim(conv_bias, x * OUTC, OUTC)[None]

    feat = swap_axes(conv_pool(pos, xpieces, wpieces, bias))
    feats = [feat, *staged_ring(feat, "x", 256)]
    feats = feats + from_other_core(feats)

    normed, qkv, mixed, partial, own, wo = forward(pos, feats, norm_gain[None], head_w)
    attended = lax.psum_scatter(partial, ("c", "x"), scatter_dimension=0, tiled=True)
    block_out = (own.astype(f32) + attended.astype(f32)).astype(bf16)
    parts = lax.all_to_all(backward(qkv, cot, wo, normed, mixed), ("zh", "y", "zl"), 0, 0)
    sums, rows = total_parts(parts)
    rows = lax.ppermute(rows, ("zh", "c", "zl"), [(0, 4), (1, 6), (2, 5), (3, 7), (4, 0), (5, 2), (6, 1), (7, 3)])
    sums, rows, block_out = lax.optimization_barrier((swap_axes(sums), rows, block_out))
    block_out = swap_axes(block_out)
    rows = jnp.stack([sums[:, 3 * HD :], rows])
    rows = jnp.stack([rows] + [lax.ppermute(rows, "y", ring(4, k)) for k in (1, 2, 3)])
    heads = lax.all_to_all(jnp.broadcast_to(sums[None, :, : 3 * HD], (8, 96, 3 * HD)), ("zl", "x"), 0, 0)
    out_grad = place_out(pos, rows, lax.ppermute(rows, "c", ring(2, 1)))
    proj_grad, block_out = lax.optimization_barrier((place_proj(heads), block_out))
    proj_grad = proj_grad.transpose(1, 0, 2)
    return (block_out[None], proj_grad, out_grad)


def solution(mesh):
    fine = Mesh(mesh.devices.reshape(2, 4, 2, 2, 4), ("zh", "y", "c", "zl", "x"))
    dp, seq = ("zh", "y", "c"), ("zl", "x")
    in_specs = (
        P(dp, seq, None),
        P(dp + seq, None, None),
        P(),
        P(),
        P(dp, None, seq),
        P(seq, dp),
        P(dp, seq, None),
    )
    out_specs = (P(dp, seq, None), P(dp, None, None), P(seq, None))
    return jax.shard_map(per_device, mesh=fine, in_specs=in_specs, out_specs=out_specs, check_vma=False)
```

```python
import jax
import jax.numpy as jnp
import numpy as np
from jax import lax
from jax.experimental import pallas as pl
from jax.experimental.pallas import tpu as pltpu
from jax.sharding import Mesh, PartitionSpec as P

HD = 192
D = 1536
NX = 4
CIN = 1408
GROUP = 44
SLOT = 48
PLANE = 32
KPAD = PLANE * SLOT
OUTC = D // NX
KW = 5
EPS = 1e-06
HALO = 16
ROWS = 1024

bf16 = jnp.bfloat16
f32 = jnp.float32


def ring(n, k):
    return [(i, (i + k) % n) for i in range(n)]


def across(low, high, axis, cut):
    far_a = lax.ppermute(lax.slice_in_dim(low, 0, cut), axis, ring(4, 1))
    far_b = lax.ppermute(lax.slice_in_dim(high, cut, None), axis, ring(4, -1))
    return far_a, far_b


def staged_ring(block, axis, cut):
    low = lax.ppermute(block, axis, ring(4, 1))
    high = lax.ppermute(block, axis, ring(4, -1))
    return low, high, *across(low, high, axis, cut)


def conv_kernel(pos_ref, *refs):
    (x0, x1, x2, x3a, x3b, w0, w1, w2, w3, o0, o1, o2, o3, bias_ref, out_ref, wcat, xs, *accs) = refs
    row = 0
    for ref in (w0, w1, w2, w3, o0, o1, o2, o3):
        for piece in range(ref.shape[0]):
            for off in range(KW):
                wcat[row : row + SLOT, off * OUTC : (off + 1) * OUTC] = ref[piece, off]
            row += SLOT
    x, half = pos_ref[1], pos_ref[3] % 2
    zeros = jnp.zeros((HALO, KPAD), bf16)
    xs[0:HALO, :] = zeros
    xs[HALO + 1024 : 2 * HALO + 1024, :] = zeros

    def place_halo(b, edge):
        @pl.when(jnp.logical_and(half == 0, b == 0))
        def _():
            xs[HALO + 1024 : 2 * HALO + 1024, :] = edge()

        @pl.when(jnp.logical_and(half == 1, b == 3))
        def _():
            xs[0:HALO, :] = edge()

    for ref, step in ((x0, 0), (x1, 3), (x2, 1)):
        b = (x + step) % NX
        xs[pl.ds(pl.multiple_of(HALO + b * 256, HALO), 256), :] = ref[0:256, :]
        place_halo(b, lambda ref=ref: ref[256 : 256 + HALO, :])
    b = (x + 2) % NX
    xs[pl.ds(pl.multiple_of(HALO + b * 256, HALO), 128), :] = x3a[...]
    xs[pl.ds(pl.multiple_of(HALO + b * 256 + 128, HALO), 128), :] = x3b[0:128, :]
    place_halo(b, lambda: x3b[128 : 128 + HALO, :])

    @pl.loop(0, 1024 // ROWS)
    def _(r):
        base = pl.multiple_of(r * ROWS, ROWS)
        y = jnp.dot(xs[pl.ds(base, ROWS + 2 * HALO), :], wcat[...], preferred_element_type=f32)
        total = bias_ref[...] + jnp.zeros((ROWS, OUTC), f32)
        for off in range(KW):
            first = HALO + off - 2
            total = total + y[first : first + ROWS, off * OUTC : (off + 1) * OUTC]
        activated = jax.nn.gelu(total)
        for n, acc in enumerate(accs):
            acc[...] = activated[:, n * 128 : (n + 1) * 128]
            top = jnp.maximum(acc[pl.ds(0, ROWS // 2, 2), :], acc[pl.ds(1, ROWS // 2, 2), :])
            out_ref[pl.ds(pl.multiple_of(r * (ROWS // 2), ROWS // 2), ROWS // 2), n * 128 : (n + 1) * 128] = top.astype(bf16)


VMEM = pl.BlockSpec(memory_space=pltpu.VMEM)
SMEM = pl.BlockSpec(memory_space=pltpu.SMEM)


def conv_pool(pos, xpieces, wpieces, bias):
    return pl.pallas_call(
        conv_kernel,
        out_shape=jax.ShapeDtypeStruct((512, OUTC), bf16),
        in_specs=[SMEM] + [VMEM] * (len(xpieces) + len(wpieces) + 1),
        out_specs=VMEM,
        scratch_shapes=[
            pltpu.VMEM((KPAD, KW * OUTC), bf16),
            pltpu.VMEM((1024 + 2 * HALO, KPAD), bf16),
            *[pltpu.VMEM((ROWS, 128), f32)] * 3,
        ],
        compiler_params=pltpu.CompilerParams(vmem_limit_bytes=48 * 1024 * 1024),
        cost_estimate=pl.CostEstimate(flops=6_000_000_000, bytes_accessed=9_000_000, transcendentals=400_000),
    )(pos, *xpieces, *wpieces, bias)


SCALE = HD ** (-0.5)
WIDE = 256
TOKENS = 1024
BLOCK = 512
NT = (((1,), (1,)), ((), ()))
TN = (((0,), (0,)), ((), ()))


def dot(a, b, dims=(((1,), (0,)), ((), ()))):
    return lax.dot_general(a, b, dims, preferred_element_type=f32)


def softmax_rows(q_block, keys):
    scores = dot(q_block, keys, NT) * SCALE
    exponent = jnp.exp(scores - jnp.max(scores, axis=-1, keepdims=True))
    return exponent * (1.0 / jnp.sum(exponent, axis=-1, keepdims=True))


def forward_kernel(pos_ref, *refs):
    feat_refs, refs = refs[:10], refs[10:]
    (gain_ref, z0, z1, z2, z3a, z3b, normed_ref, qkv_ref, mixed_ref, partial_ref, own_ref, wo, feats, wq) = refs
    c, x, z = pos_ref[0], pos_ref[1], pos_ref[3]
    for t in range(3):
        wq[:, t * WIDE + HD : (t + 1) * WIDE] = jnp.zeros((D, WIDE - HD), bf16)
    wo[:, HD:] = jnp.zeros((D, WIDE - HD), bf16)
    for ref, zstep, first in ((z0, 0, 0), (z1, 3, 0), (z2, 1, 0), (z3a, 2, 0), (z3b, 2, 2)):
        for k in range(ref.shape[0]):
            src_z, src_y = (z + zstep) % 4, first + k
            rows = pl.ds(pl.multiple_of((((src_z // 2) * 4 + src_y) * 2 + src_z % 2) * 96, 96), 96)
            piece = ref[k]
            for t in range(3):
                wq[rows, t * WIDE : t * WIDE + HD] = piece[:, t * HD : (t + 1) * HD]
            wo[rows, :HD] = piece[:, 3 * HD :]

    for side in range(2):
        half = c if side == 0 else 1 - c
        for ref, step, first in zip(feat_refs[side * 5 : side * 5 + 5], (0, 3, 1, 2, 2), (0, 0, 0, 0, 256)):
            size = ref.shape[0]
            rows = pl.ds(pl.multiple_of(half * 512 + first, 256), size)
            lanes = pl.ds(pl.multiple_of(((x + step) % NX) * OUTC, 128), OUTC)
            feats[rows, lanes] = ref[...]
    own_ref[...] = feats[pl.ds(pl.multiple_of((c * NX + x) * 128, 128), 128), :]

    @pl.loop(0, TOKENS // BLOCK)
    def _(r):
        rows = pl.ds(pl.multiple_of(r * BLOCK, BLOCK), BLOCK)
        part = feats[rows, :].astype(f32)
        factor = lax.rsqrt(jnp.sum(part * part, axis=-1, keepdims=True) * (1.0 / D) + EPS)
        normed = (part * factor * gain_ref[...]).astype(bf16)
        normed_ref[rows, :] = normed
        qkv = dot(normed, wq[...]).astype(bf16)
        for t in range(3):
            qkv_ref[t, rows, :] = qkv[:, t * WIDE : (t + 1) * WIDE]

    @pl.loop(0, TOKENS // BLOCK)
    def _(r):
        rows = pl.ds(pl.multiple_of(r * BLOCK, BLOCK), BLOCK)
        weights = softmax_rows(qkv_ref[0, rows, :], qkv_ref[1]).astype(bf16)
        mixed = dot(weights, qkv_ref[2]).astype(bf16)
        mixed_ref[rows, :] = mixed
        partial_ref[rows, :] = dot(mixed, wo[...], NT).astype(bf16)


def forward(pos, feats, gain, wpieces):
    return pl.pallas_call(
        forward_kernel,
        out_shape=(
            jax.ShapeDtypeStruct((TOKENS, D), bf16),
            jax.ShapeDtypeStruct((3, TOKENS, WIDE), bf16),
            jax.ShapeDtypeStruct((TOKENS, WIDE), bf16),
            jax.ShapeDtypeStruct((TOKENS, D), bf16),
            jax.ShapeDtypeStruct((128, D), bf16),
            jax.ShapeDtypeStruct((D, WIDE), bf16),
        ),
        in_specs=[SMEM] + [VMEM] * 16,
        out_specs=[VMEM] * 6,
        scratch_shapes=[pltpu.VMEM((TOKENS, D), bf16), pltpu.VMEM((D, 3 * WIDE), bf16)],
        compiler_params=pltpu.CompilerParams(vmem_limit_bytes=48 * 1024 * 1024),
        cost_estimate=pl.CostEstimate(flops=4_000_000_000, bytes_accessed=16_000_000, transcendentals=1_100_000),
    )(pos, *feats, gain, *wpieces)


def backward_kernel(
    qkv_ref, cot_ref, wo, normed_ref, mixed_ref, sent_ref, dcat, dk, dv, grads, outs
):
    @pl.loop(0, TOKENS // BLOCK)
    def _(r):
        rows = pl.ds(pl.multiple_of(r * BLOCK, BLOCK), BLOCK)
        d_mixed = dot(cot_ref[rows, :], wo[...]).astype(bf16)
        q_block = qkv_ref[0, rows, :]
        weights = softmax_rows(q_block, qkv_ref[1])
        d_weights = dot(d_mixed, qkv_ref[2], NT)
        centre = jnp.sum(weights * d_weights, axis=-1, keepdims=True)
        d_scores = (weights * (d_weights - centre) * SCALE).astype(bf16)
        dcat[rows, 0:HD] = dot(d_scores, qkv_ref[1]).astype(bf16)[:, :HD]
        d_value = dot(d_mixed, weights.astype(bf16), TN)
        d_key = dot(q_block, d_scores, TN)

        @pl.when(r == 0)
        def _():
            dv[...] = d_value
            dk[...] = d_key

        @pl.when(r > 0)
        def _():
            dv[...] += d_value
            dk[...] += d_key

    dcat[:, HD : 2 * HD] = dk[...].T.astype(bf16)[:, :HD]
    dcat[:, 2 * HD : 3 * HD] = dv[...].T.astype(bf16)[:, :HD]

    @pl.loop(0, 2)
    def _(n):
        lanes = pl.ds(pl.multiple_of(n * 768, 768), 768)
        grads[lanes, :] = dot(normed_ref[:, lanes], dcat[...], TN)
        outs[:, lanes] = dot(mixed_ref[...], cot_ref[:, lanes], TN)[:HD]

    for d in range(16):
        sent_ref[d, :, : 3 * HD] = grads[d * 96 : (d + 1) * 96, :].astype(bf16)
        g, lane = d // 2, (d % 2) * 768
        packed = [outs[g * 24 : (g + 1) * 24, lane + j * HD : lane + (j + 1) * HD] for j in range(4)]
        sent_ref[d, :, 3 * HD :] = jnp.concatenate(packed, axis=0).astype(bf16)


def backward(qkv, cot, wo, normed, mixed):
    return pl.pallas_call(
        backward_kernel,
        out_shape=jax.ShapeDtypeStruct((16, 96, 768), bf16),
        in_specs=[VMEM] * 5,
        out_specs=VMEM,
        scratch_shapes=[
            pltpu.VMEM((TOKENS, 3 * HD), bf16),
            pltpu.VMEM((WIDE, TOKENS), f32),
            pltpu.VMEM((WIDE, TOKENS), f32),
            pltpu.VMEM((D, 3 * HD), f32),
            pltpu.VMEM((HD, D), f32),
        ],
        compiler_params=pltpu.CompilerParams(vmem_limit_bytes=56 * 1024 * 1024),
        cost_estimate=pl.CostEstimate(flops=6_000_000_000, bytes_accessed=18_000_000, transcendentals=1_100_000),
    )(qkv, cot, wo, normed, mixed)


def total_kernel(parts_ref, out_ref, rows_ref):
    total = parts_ref[0].astype(f32)
    for g in range(1, 16):
        total = total + parts_ref[g].astype(f32)
    out_ref[...] = total.astype(bf16)
    rows_ref[...] = total[:, 3 * HD :].astype(bf16)


def total_parts(parts):
    return pl.pallas_call(
        total_kernel,
        out_shape=(jax.ShapeDtypeStruct((96, 768), bf16), jax.ShapeDtypeStruct((96, HD), bf16)),
        in_specs=[VMEM],
        out_specs=[VMEM] * 2,
    )(parts)


def proj_kernel(heads_ref, out_ref):
    for h in range(8):
        for t in range(3):
            out_ref[t, :, h * HD : (h + 1) * HD] = heads_ref[h, :, t * HD : (t + 1) * HD].astype(f32)


def place_proj(heads):
    return pl.pallas_call(
        proj_kernel,
        out_shape=jax.ShapeDtypeStruct((3, 96, D), f32),
        in_specs=[VMEM],
        out_specs=VMEM,
    )(heads)


def out_kernel(pos_ref, own_ref, other_ref, out_ref):
    c, y, zh = pos_ref[0], pos_ref[2], pos_ref[3] // 2
    for ref, core in ((own_ref, c), (other_ref, 1 - c)):
        lanes = pl.ds(pl.multiple_of(core * 768, 768), 768)
        for step in range(2):
            for k in range(4):
                g = ((zh + step) % 2) * 4 + (y + 4 - k) % 4
                piece = [ref[k, step, j * 24 : (j + 1) * 24, :] for j in range(4)]
                rows = pl.ds(pl.multiple_of(g * 24, 8), 24)
                out_ref[rows, lanes] = jnp.concatenate(piece, axis=1).astype(f32)


def place_out(pos, own, other):
    return pl.pallas_call(
        out_kernel,
        out_shape=jax.ShapeDtypeStruct((HD, D), f32),
        in_specs=[SMEM, VMEM, VMEM],
        out_specs=VMEM,
    )(pos, own, other)


def lane_sources(zh, y, c, zl):
    lane = lax.iota(jnp.int32, KPAD)
    slot, j = lane // SLOT, lane % SLOT
    core = jnp.where(slot < 16, c, 1 - c)
    within = slot % 16
    zstep = within // 4
    ystep = within % 4
    z = zh * 2 + zl
    src_z = (z + jnp.where(zstep == 1, 3, jnp.where(zstep == 2, 1, jnp.where(zstep == 3, 2, 0)))) % 4
    src_y = (y + 4 - ystep) % 4
    plane = (((src_z // 2) * 4 + src_y) * 2 + core) * 2 + src_z % 2
    return jnp.where(j < GROUP, plane * GROUP + j, -1)


def lanes_kernel(block_ref, edge_ref, sources_ref, out_ref):
    for n in range(4):
        lanes = slice(n * 384, (n + 1) * 384)
        select = lax.broadcasted_iota(jnp.int32, (CIN, 384), 0) == sources_ref[:, lanes]
        select = jnp.where(select, 1.0, 0.0).astype(bf16)
        out_ref[0:256, lanes] = dot(block_ref[...], select).astype(bf16)
        out_ref[256:, lanes] = dot(edge_ref[...], select).astype(bf16)


def order_lanes(block, edge, sources):
    return pl.pallas_call(
        lanes_kernel,
        out_shape=jax.ShapeDtypeStruct((256 + HALO, KPAD), bf16),
        in_specs=[VMEM] * 3,
        out_specs=VMEM,
        compiler_params=pltpu.CompilerParams(vmem_limit_bytes=32 * 1024 * 1024),
        cost_estimate=pl.CostEstimate(flops=1_200_000_000, bytes_accessed=1_600_000, transcendentals=0),
    )(block, edge, sources)


def swap_axes(value):
    return lax.ppermute(value, ("c", "zl"), [(0, 0), (1, 2), (2, 1), (3, 3)])


def from_other_core(parts):
    return [lax.ppermute(p, "c", ring(2, 1)) for p in parts]


def per_device(sequence, conv_weight, conv_bias, norm_gain, proj_weight, out_weight, cotangent):
    zh, y, c, zl, x = (lax.axis_index(a) for a in ("zh", "y", "c", "zl", "x"))
    zring = ("zh", "zl")
    pos = jnp.stack([c, x, y, zh * 2 + zl])

    edge = jnp.where(zl == 0, sequence[0, -HALO:], sequence[0, :HALO])
    edge = lax.ppermute(edge, "zl", ring(2, 1))
    block = order_lanes(sequence[0], edge, lane_sources(zh, y, c, zl)[None])

    split = conv_weight.reshape(11, KW, NX, OUTC).transpose(2, 1, 0, 3)
    mine = jnp.zeros((NX, KW, 11, OUTC), bf16)
    for k in range(NX):
        piece = lax.dynamic_index_in_dim(split, (x + k) % NX, 0, keepdims=False)
        if k:
            piece = lax.ppermute(piece, "x", ring(NX, k))
        mine = lax.dynamic_update_index_in_dim(mine, piece, (x + NX - k) % NX, 0)
    mine = mine.transpose(1, 0, 2, 3).reshape(KW, GROUP, OUTC)
    mine = jnp.pad(mine, ((0, 0), (0, SLOT - GROUP), (0, 0)))

    later = jnp.concatenate([proj_weight.reshape(96, 3 * HD), out_weight.T], axis=1).reshape(48, D)
    later = swap_axes(jnp.concatenate([cotangent[0], later], axis=0))

    head_w = lax.all_gather(later[128:].reshape(96, 768), "y", axis=0)

    ypieces = [mine] + [lax.ppermute(mine, "y", ring(4, k)) for k in (1, 2, 3)]
    *ypieces, block = lax.optimization_barrier((*ypieces, block))
    ypieces = jnp.stack(ypieces)
    zpieces = [lax.ppermute(ypieces, zring, ring(4, k)) for k in (1, -1, 2)]
    xlow, xhigh = (lax.ppermute(block, "x", ring(4, k)) for k in (1, -1))
    yother = lax.ppermute(ypieces, "c", ring(2, 1))
    zpieces[0], xlow, xhigh, yother = lax.optimization_barrier((zpieces[0], xlow, xhigh, yother))
    xfar = across(xlow, xhigh, "x", 128)
    zothers = from_other_core(zpieces[:2])
    *zpieces, xa, xb, za, zb, head_w, cot = lax.optimization_barrier((*zpieces, *xfar, *zothers, head_w, later[:128]))
    cot = lax.all_gather(cot, ("c", "x"), axis=0, tiled=True)
    xpieces = [block, xlow, xhigh, xa, xb]
    wpieces = [ypieces, *zpieces, yother, za, zb, *from_other_core(zpieces[2:])]
    head_w = [head_w, *staged_ring(head_w, zring, 2)]
    bias = lax.dynamic_slice_in_dim(conv_bias, x * OUTC, OUTC)[None]

    feat = swap_axes(conv_pool(pos, xpieces, wpieces, bias))
    feats = [feat, *staged_ring(feat, "x", 256)]
    feats = feats + from_other_core(feats)

    normed, qkv, mixed, partial, own, wo = forward(pos, feats, norm_gain[None], head_w)
    attended = lax.psum_scatter(partial, ("c", "x"), scatter_dimension=0, tiled=True)
    block_out = (own.astype(f32) + attended.astype(f32)).astype(bf16)
    parts = lax.all_to_all(backward(qkv, cot, wo, normed, mixed), ("zh", "y", "zl"), 0, 0)
    sums, rows = total_parts(parts)
    rows = lax.ppermute(rows, ("zh", "c", "zl"), [(0, 4), (1, 6), (2, 5), (3, 7), (4, 0), (5, 2), (6, 1), (7, 3)])
    sums, rows, block_out = lax.optimization_barrier((swap_axes(sums), rows, block_out))
    block_out = swap_axes(block_out)
    rows = jnp.stack([sums[:, 3 * HD :], rows])
    rows = jnp.stack([rows] + [lax.ppermute(rows, "y", ring(4, k)) for k in (1, 2, 3)])
    heads = lax.all_to_all(jnp.broadcast_to(sums[None, :, : 3 * HD], (8, 96, 3 * HD)), ("zl", "x"), 0, 0)
    out_grad = place_out(pos, rows, lax.ppermute(rows, "c", ring(2, 1)))
    proj_grad, block_out = lax.optimization_barrier((place_proj(heads), block_out))
    proj_grad = proj_grad.transpose(1, 0, 2)
    return (block_out[None], proj_grad, out_grad)


def solution(mesh):
    fine = Mesh(mesh.devices.reshape(2, 4, 2, 2, 4), ("zh", "y", "c", "zl", "x"))
    dp, seq = ("zh", "y", "c"), ("zl", "x")
    in_specs = (
        P(dp, seq, None),
        P(dp + seq, None, None),
        P(),
        P(),
        P(dp, None, seq),
        P(seq, dp),
        P(dp, seq, None),
    )
    out_specs = (P(dp, seq, None), P(dp, None, None), P(seq, None))
    return jax.shard_map(per_device, mesh=fine, in_specs=in_specs, out_specs=out_specs, check_vma=False)
```

```python
import jax
import jax.numpy as jnp
import numpy as np
from jax import lax
from jax.experimental import pallas as pl
from jax.experimental.pallas import tpu as pltpu
from jax.sharding import Mesh, PartitionSpec as P

HD = 192
D = 1536
NX = 4
CIN = 1408
GROUP = 44
SLOT = 48
PLANE = 32
KPAD = PLANE * SLOT
OUTC = D // NX
KW = 5
EPS = 1e-06
HALO = 16
ROWS = 1024

bf16 = jnp.bfloat16
f32 = jnp.float32


def ring(n, k):
    return [(i, (i + k) % n) for i in range(n)]


def across(low, high, axis, cut):
    far_a = lax.ppermute(lax.slice_in_dim(low, 0, cut), axis, ring(4, 1))
    far_b = lax.ppermute(lax.slice_in_dim(high, cut, None), axis, ring(4, -1))
    return far_a, far_b


def staged_ring(block, axis, cut):
    low = lax.ppermute(block, axis, ring(4, 1))
    high = lax.ppermute(block, axis, ring(4, -1))
    return low, high, *across(low, high, axis, cut)


def conv_kernel(pos_ref, *refs):
    (x0, x1, x2, x3a, x3b, w0, w1, w2, w3, o0, o1, o2, o3, bias_ref, out_ref, wcat, xs, *accs) = refs
    row = 0
    for ref in (w0, w1, w2, w3, o0, o1, o2, o3):
        for piece in range(ref.shape[0]):
            for off in range(KW):
                wcat[row : row + SLOT, off * OUTC : (off + 1) * OUTC] = ref[piece, off]
            row += SLOT
    x, half = pos_ref[1], pos_ref[3] % 2
    zeros = jnp.zeros((HALO, KPAD), bf16)
    xs[0:HALO, :] = zeros
    xs[HALO + 1024 : 2 * HALO + 1024, :] = zeros

    def place_halo(b, edge):
        @pl.when(jnp.logical_and(half == 0, b == 0))
        def _():
            xs[HALO + 1024 : 2 * HALO + 1024, :] = edge()

        @pl.when(jnp.logical_and(half == 1, b == 3))
        def _():
            xs[0:HALO, :] = edge()

    for ref, step in ((x0, 0), (x1, 3), (x2, 1)):
        b = (x + step) % NX
        xs[pl.ds(pl.multiple_of(HALO + b * 256, HALO), 256), :] = ref[0:256, :]
        place_halo(b, lambda ref=ref: ref[256 : 256 + HALO, :])
    b = (x + 2) % NX
    xs[pl.ds(pl.multiple_of(HALO + b * 256, HALO), 128), :] = x3a[...]
    xs[pl.ds(pl.multiple_of(HALO + b * 256 + 128, HALO), 128), :] = x3b[0:128, :]
    place_halo(b, lambda: x3b[128 : 128 + HALO, :])

    @pl.loop(0, 1024 // ROWS)
    def _(r):
        base = pl.multiple_of(r * ROWS, ROWS)
        y = jnp.dot(xs[pl.ds(base, ROWS + 2 * HALO), :], wcat[...], preferred_element_type=f32)
        total = bias_ref[...] + jnp.zeros((ROWS, OUTC), f32)
        for off in range(KW):
            first = HALO + off - 2
            total = total + y[first : first + ROWS, off * OUTC : (off + 1) * OUTC]
        activated = jax.nn.gelu(total)
        for n, acc in enumerate(accs):
            acc[...] = activated[:, n * 128 : (n + 1) * 128]
            top = jnp.maximum(acc[pl.ds(0, ROWS // 2, 2), :], acc[pl.ds(1, ROWS // 2, 2), :])
            out_ref[pl.ds(pl.multiple_of(r * (ROWS // 2), ROWS // 2), ROWS // 2), n * 128 : (n + 1) * 128] = top.astype(bf16)


VMEM = pl.BlockSpec(memory_space=pltpu.VMEM)
SMEM = pl.BlockSpec(memory_space=pltpu.SMEM)


def conv_pool(pos, xpieces, wpieces, bias):
    return pl.pallas_call(
        conv_kernel,
        out_shape=jax.ShapeDtypeStruct((512, OUTC), bf16),
        in_specs=[SMEM] + [VMEM] * (len(xpieces) + len(wpieces) + 1),
        out_specs=VMEM,
        scratch_shapes=[
            pltpu.VMEM((KPAD, KW * OUTC), bf16),
            pltpu.VMEM((1024 + 2 * HALO, KPAD), bf16),
            *[pltpu.VMEM((ROWS, 128), f32)] * 3,
        ],
        compiler_params=pltpu.CompilerParams(vmem_limit_bytes=48 * 1024 * 1024),
        cost_estimate=pl.CostEstimate(flops=6_000_000_000, bytes_accessed=9_000_000, transcendentals=400_000),
    )(pos, *xpieces, *wpieces, bias)


SCALE = HD ** (-0.5)
WIDE = 256
TOKENS = 1024
BLOCK = 512
NT = (((1,), (1,)), ((), ()))
TN = (((0,), (0,)), ((), ()))


def dot(a, b, dims=(((1,), (0,)), ((), ()))):
    return lax.dot_general(a, b, dims, preferred_element_type=f32)


def softmax_rows(q_block, keys):
    scores = dot(q_block, keys, NT) * SCALE
    exponent = jnp.exp(scores - jnp.max(scores, axis=-1, keepdims=True))
    return exponent * (1.0 / jnp.sum(exponent, axis=-1, keepdims=True))


def forward_kernel(pos_ref, *refs):
    feat_refs, refs = refs[:10], refs[10:]
    (gain_ref, z0, z1, z2, z3a, z3b, normed_ref, qkv_ref, mixed_ref, partial_ref, own_ref, wo, feats, wq) = refs
    c, x, z = pos_ref[0], pos_ref[1], pos_ref[3]
    for t in range(3):
        wq[:, t * WIDE + HD : (t + 1) * WIDE] = jnp.zeros((D, WIDE - HD), bf16)
    wo[:, HD:] = jnp.zeros((D, WIDE - HD), bf16)
    for ref, zstep, first in ((z0, 0, 0), (z1, 3, 0), (z2, 1, 0), (z3a, 2, 0), (z3b, 2, 2)):
        for k in range(ref.shape[0]):
            src_z, src_y = (z + zstep) % 4, first + k
            rows = pl.ds(pl.multiple_of((((src_z // 2) * 4 + src_y) * 2 + src_z % 2) * 96, 96), 96)
            piece = ref[k]
            for t in range(3):
                wq[rows, t * WIDE : t * WIDE + HD] = piece[:, t * HD : (t + 1) * HD]
            wo[rows, :HD] = piece[:, 3 * HD :]

    for side in range(2):
        half = c if side == 0 else 1 - c
        for ref, step, first in zip(feat_refs[side * 5 : side * 5 + 5], (0, 3, 1, 2, 2), (0, 0, 0, 0, 256)):
            size = ref.shape[0]
            rows = pl.ds(pl.multiple_of(half * 512 + first, 256), size)
            lanes = pl.ds(pl.multiple_of(((x + step) % NX) * OUTC, 128), OUTC)
            feats[rows, lanes] = ref[...]
    own_ref[...] = feats[pl.ds(pl.multiple_of((c * NX + x) * 128, 128), 128), :]

    @pl.loop(0, TOKENS // BLOCK)
    def _(r):
        rows = pl.ds(pl.multiple_of(r * BLOCK, BLOCK), BLOCK)
        part = feats[rows, :].astype(f32)
        factor = lax.rsqrt(jnp.sum(part * part, axis=-1, keepdims=True) * (1.0 / D) + EPS)
        normed = (part * factor * gain_ref[...]).astype(bf16)
        normed_ref[rows, :] = normed
        qkv = dot(normed, wq[...]).astype(bf16)
        for t in range(3):
            qkv_ref[t, rows, :] = qkv[:, t * WIDE : (t + 1) * WIDE]

    @pl.loop(0, TOKENS // BLOCK)
    def _(r):
        rows = pl.ds(pl.multiple_of(r * BLOCK, BLOCK), BLOCK)
        weights = softmax_rows(qkv_ref[0, rows, :], qkv_ref[1]).astype(bf16)
        mixed = dot(weights, qkv_ref[2]).astype(bf16)
        mixed_ref[rows, :] = mixed
        partial_ref[rows, :] = dot(mixed, wo[...], NT).astype(bf16)


def forward(pos, feats, gain, wpieces):
    return pl.pallas_call(
        forward_kernel,
        out_shape=(
            jax.ShapeDtypeStruct((TOKENS, D), bf16),
            jax.ShapeDtypeStruct((3, TOKENS, WIDE), bf16),
            jax.ShapeDtypeStruct((TOKENS, WIDE), bf16),
            jax.ShapeDtypeStruct((TOKENS, D), bf16),
            jax.ShapeDtypeStruct((128, D), bf16),
            jax.ShapeDtypeStruct((D, WIDE), bf16),
        ),
        in_specs=[SMEM] + [VMEM] * 16,
        out_specs=[VMEM] * 6,
        scratch_shapes=[pltpu.VMEM((TOKENS, D), bf16), pltpu.VMEM((D, 3 * WIDE), bf16)],
        compiler_params=pltpu.CompilerParams(vmem_limit_bytes=48 * 1024 * 1024),
        cost_estimate=pl.CostEstimate(flops=4_000_000_000, bytes_accessed=16_000_000, transcendentals=1_100_000),
    )(pos, *feats, gain, *wpieces)


def backward_kernel(
    qkv_ref, cot_ref, wo, normed_ref, mixed_ref, sent_ref, dcat, dk, dv, grads, outs
):
    @pl.loop(0, TOKENS // BLOCK)
    def _(r):
        rows = pl.ds(pl.multiple_of(r * BLOCK, BLOCK), BLOCK)
        d_mixed = dot(cot_ref[rows, :], wo[...]).astype(bf16)
        q_block = qkv_ref[0, rows, :]
        weights = softmax_rows(q_block, qkv_ref[1])
        d_weights = dot(d_mixed, qkv_ref[2], NT)
        centre = jnp.sum(weights * d_weights, axis=-1, keepdims=True)
        d_scores = (weights * (d_weights - centre) * SCALE).astype(bf16)
        dcat[rows, 0:HD] = dot(d_scores, qkv_ref[1]).astype(bf16)[:, :HD]
        d_value = dot(d_mixed, weights.astype(bf16), TN)
        d_key = dot(q_block, d_scores, TN)

        @pl.when(r == 0)
        def _():
            dv[...] = d_value
            dk[...] = d_key

        @pl.when(r > 0)
        def _():
            dv[...] += d_value
            dk[...] += d_key

    dcat[:, HD : 2 * HD] = dk[...].T.astype(bf16)[:, :HD]
    dcat[:, 2 * HD : 3 * HD] = dv[...].T.astype(bf16)[:, :HD]

    outs[...] = dot(mixed_ref[...], cot_ref[...], TN)[:HD]
    grads[...] = dot(normed_ref[...], dcat[...], TN)

    for d in range(16):
        sent_ref[d, :, : 3 * HD] = grads[d * 96 : (d + 1) * 96, :].astype(bf16)
        g, lane = d // 2, (d % 2) * 768
        packed = [outs[g * 24 : (g + 1) * 24, lane + j * HD : lane + (j + 1) * HD] for j in range(4)]
        sent_ref[d, :, 3 * HD :] = jnp.concatenate(packed, axis=0).astype(bf16)


def backward(qkv, cot, wo, normed, mixed):
    return pl.pallas_call(
        backward_kernel,
        out_shape=jax.ShapeDtypeStruct((16, 96, 768), bf16),
        in_specs=[VMEM] * 5,
        out_specs=VMEM,
        scratch_shapes=[
            pltpu.VMEM((TOKENS, 3 * HD), bf16),
            pltpu.VMEM((WIDE, TOKENS), f32),
            pltpu.VMEM((WIDE, TOKENS), f32),
            pltpu.VMEM((D, 3 * HD), f32),
            pltpu.VMEM((HD, D), f32),
        ],
        compiler_params=pltpu.CompilerParams(vmem_limit_bytes=56 * 1024 * 1024),
        cost_estimate=pl.CostEstimate(flops=6_000_000_000, bytes_accessed=18_000_000, transcendentals=1_100_000),
    )(qkv, cot, wo, normed, mixed)


def total_kernel(parts_ref, out_ref, rows_ref):
    total = parts_ref[0].astype(f32)
    for g in range(1, 16):
        total = total + parts_ref[g].astype(f32)
    out_ref[...] = total.astype(bf16)
    rows_ref[...] = total[:, 3 * HD :].astype(bf16)


def total_parts(parts):
    return pl.pallas_call(
        total_kernel,
        out_shape=(jax.ShapeDtypeStruct((96, 768), bf16), jax.ShapeDtypeStruct((96, HD), bf16)),
        in_specs=[VMEM],
        out_specs=[VMEM] * 2,
    )(parts)


def proj_kernel(heads_ref, out_ref):
    for h in range(8):
        for t in range(3):
            out_ref[t, :, h * HD : (h + 1) * HD] = heads_ref[h, :, t * HD : (t + 1) * HD].astype(f32)


def place_proj(heads):
    return pl.pallas_call(
        proj_kernel,
        out_shape=jax.ShapeDtypeStruct((3, 96, D), f32),
        in_specs=[VMEM],
        out_specs=VMEM,
    )(heads)


def out_kernel(pos_ref, own_ref, other_ref, out_ref):
    c, y, zh = pos_ref[0], pos_ref[2], pos_ref[3] // 2
    for ref, core in ((own_ref, c), (other_ref, 1 - c)):
        lanes = pl.ds(pl.multiple_of(core * 768, 768), 768)
        for step in range(2):
            for k in range(4):
                g = ((zh + step) % 2) * 4 + (y + 4 - k) % 4
                piece = [ref[k, step, j * 24 : (j + 1) * 24, :] for j in range(4)]
                rows = pl.ds(pl.multiple_of(g * 24, 8), 24)
                out_ref[rows, lanes] = jnp.concatenate(piece, axis=1).astype(f32)


def place_out(pos, own, other):
    return pl.pallas_call(
        out_kernel,
        out_shape=jax.ShapeDtypeStruct((HD, D), f32),
        in_specs=[SMEM, VMEM, VMEM],
        out_specs=VMEM,
    )(pos, own, other)


def lane_sources(zh, y, c, zl):
    lane = lax.iota(jnp.int32, KPAD)
    slot, j = lane // SLOT, lane % SLOT
    core = jnp.where(slot < 16, c, 1 - c)
    within = slot % 16
    zstep = within // 4
    ystep = within % 4
    z = zh * 2 + zl
    src_z = (z + jnp.where(zstep == 1, 3, jnp.where(zstep == 2, 1, jnp.where(zstep == 3, 2, 0)))) % 4
    src_y = (y + 4 - ystep) % 4
    plane = (((src_z // 2) * 4 + src_y) * 2 + core) * 2 + src_z % 2
    return jnp.where(j < GROUP, plane * GROUP + j, -1)


def lanes_kernel(block_ref, edge_ref, sources_ref, out_ref):
    for n in range(4):
        lanes = slice(n * 384, (n + 1) * 384)
        select = lax.broadcasted_iota(jnp.int32, (CIN, 384), 0) == sources_ref[:, lanes]
        select = jnp.where(select, 1.0, 0.0).astype(bf16)
        out_ref[0:256, lanes] = dot(block_ref[...], select).astype(bf16)
        out_ref[256:, lanes] = dot(edge_ref[...], select).astype(bf16)


def order_lanes(block, edge, sources):
    return pl.pallas_call(
        lanes_kernel,
        out_shape=jax.ShapeDtypeStruct((256 + HALO, KPAD), bf16),
        in_specs=[VMEM] * 3,
        out_specs=VMEM,
        compiler_params=pltpu.CompilerParams(vmem_limit_bytes=32 * 1024 * 1024),
        cost_estimate=pl.CostEstimate(flops=1_200_000_000, bytes_accessed=1_600_000, transcendentals=0),
    )(block, edge, sources)


def swap_axes(value):
    return lax.ppermute(value, ("c", "zl"), [(0, 0), (1, 2), (2, 1), (3, 3)])


def from_other_core(parts):
    return [lax.ppermute(p, "c", ring(2, 1)) for p in parts]


def per_device(sequence, conv_weight, conv_bias, norm_gain, proj_weight, out_weight, cotangent):
    zh, y, c, zl, x = (lax.axis_index(a) for a in ("zh", "y", "c", "zl", "x"))
    zring = ("zh", "zl")
    pos = jnp.stack([c, x, y, zh * 2 + zl])

    edge = jnp.where(zl == 0, sequence[0, -HALO:], sequence[0, :HALO])
    edge = lax.ppermute(edge, "zl", ring(2, 1))
    block = order_lanes(sequence[0], edge, lane_sources(zh, y, c, zl)[None])

    split = conv_weight.reshape(11, KW, NX, OUTC).transpose(2, 1, 0, 3)
    mine = jnp.zeros((NX, KW, 11, OUTC), bf16)
    for k in range(NX):
        piece = lax.dynamic_index_in_dim(split, (x + k) % NX, 0, keepdims=False)
        if k:
            piece = lax.ppermute(piece, "x", ring(NX, k))
        mine = lax.dynamic_update_index_in_dim(mine, piece, (x + NX - k) % NX, 0)
    mine = mine.transpose(1, 0, 2, 3).reshape(KW, GROUP, OUTC)
    mine = jnp.pad(mine, ((0, 0), (0, SLOT - GROUP), (0, 0)))

    later = jnp.concatenate([proj_weight.reshape(96, 3 * HD), out_weight.T], axis=1).reshape(48, D)
    later = swap_axes(jnp.concatenate([cotangent[0], later], axis=0))

    head_w = lax.all_gather(later[128:].reshape(96, 768), "y", axis=0)

    ypieces = [mine] + [lax.ppermute(mine, "y", ring(4, k)) for k in (1, 2, 3)]
    *ypieces, block = lax.optimization_barrier((*ypieces, block))
    ypieces = jnp.stack(ypieces)
    zpieces = [lax.ppermute(ypieces, zring, ring(4, k)) for k in (1, -1, 2)]
    xlow, xhigh = (lax.ppermute(block, "x", ring(4, k)) for k in (1, -1))
    yother = lax.ppermute(ypieces, "c", ring(2, 1))
    zpieces[0], xlow, xhigh, yother = lax.optimization_barrier((zpieces[0], xlow, xhigh, yother))
    xfar = across(xlow, xhigh, "x", 128)
    zothers = from_other_core(zpieces[:2])
    *zpieces, xa, xb, za, zb, head_w, cot = lax.optimization_barrier((*zpieces, *xfar, *zothers, head_w, later[:128]))
    cot = lax.all_gather(cot, ("c", "x"), axis=0, tiled=True)
    xpieces = [block, xlow, xhigh, xa, xb]
    wpieces = [ypieces, *zpieces, yother, za, zb, *from_other_core(zpieces[2:])]
    head_w = [head_w, *staged_ring(head_w, zring, 2)]
    bias = lax.dynamic_slice_in_dim(conv_bias, x * OUTC, OUTC)[None]

    feat = swap_axes(conv_pool(pos, xpieces, wpieces, bias))
    feats = [feat, *staged_ring(feat, "x", 256)]
    feats = feats + from_other_core(feats)

    normed, qkv, mixed, partial, own, wo = forward(pos, feats, norm_gain[None], head_w)
    attended = lax.psum_scatter(partial, ("c", "x"), scatter_dimension=0, tiled=True)
    block_out = (own.astype(f32) + attended.astype(f32)).astype(bf16)
    parts = lax.all_to_all(backward(qkv, cot, wo, normed, mixed), ("zh", "y", "zl"), 0, 0)
    sums, rows = total_parts(parts)
    rows = lax.ppermute(rows, ("zh", "c", "zl"), [(0, 4), (1, 6), (2, 5), (3, 7), (4, 0), (5, 2), (6, 1), (7, 3)])
    sums, rows, block_out = lax.optimization_barrier((swap_axes(sums), rows, block_out))
    block_out = swap_axes(block_out)
    rows = jnp.stack([sums[:, 3 * HD :], rows])
    rows = jnp.stack([rows] + [lax.ppermute(rows, "y", ring(4, k)) for k in (1, 2, 3)])
    heads = lax.all_to_all(jnp.broadcast_to(sums[None, :, : 3 * HD], (8, 96, 3 * HD)), ("zl", "x"), 0, 0)
    out_grad = place_out(pos, rows, lax.ppermute(rows, "c", ring(2, 1)))
    proj_grad, block_out = lax.optimization_barrier((place_proj(heads), block_out))
    proj_grad = proj_grad.transpose(1, 0, 2)
    return (block_out[None], proj_grad, out_grad)


def solution(mesh):
    fine = Mesh(mesh.devices.reshape(2, 4, 2, 2, 4), ("zh", "y", "c", "zl", "x"))
    dp, seq = ("zh", "y", "c"), ("zl", "x")
    in_specs = (
        P(dp, seq, None),
        P(dp + seq, None, None),
        P(),
        P(),
        P(dp, None, seq),
        P(seq, dp),
        P(dp, seq, None),
    )
    out_specs = (P(dp, seq, None), P(dp, None, None), P(seq, None))
    return jax.shard_map(per_device, mesh=fine, in_specs=in_specs, out_specs=out_specs, check_vma=False)
```
